32 devices in a mesh: parts: 1, uly: 8 (over z, x), blk: 4 (over y, core).
Axes of the slice: x: 2, y: 2, z: 4, core: 2. Of those that a mesh axis runs over, the one named last changes fastest.
Arguments:
- queries: bfloat16 [4, 512, 8192], P(('parts', 'blk'), 'uly'), may hold values from -4.5 to 4.5
- keys: bfloat16 [4, 512, 1024], P(('parts', 'blk'), 'uly'), may hold values from -4.5 to 4.5
- values: bfloat16 [4, 512, 1024], P(('parts', 'blk'), 'uly'), may hold values from -6 to 6
- doc_blocks: int32 [4], P('parts'), may hold values from 1 to 12, 16 in all
Outputs:
- attended: bfloat16 [4, 512, 8192], P(('parts', 'blk'), 'uly')
The draws below stay inside these ranges and needn't reach their ends.
Inputs may be any that keep to these rules, and one draw needn't show every extreme that they name: `doc_blocks`: the lengths sum to 16; the longest document holds exactly (3) * 512 tokens.
All inputs are finite; a program needn't handle non-finite values.
Results may differ from the reference program's by a relative error of at most 0.0037.
Values may be sent and summed in bfloat16 or wider, within the bound.
A program may use at most 128 MiB of HBM per device.

```python
import math
import jax
import jax.numpy as jnp
import numpy as np
from jax import lax

QUERY_HEADS = 64
KEY_VALUE_HEADS = 8
HEAD_WIDTH = 128
BLOCK = 128
BLOCK_TOKENS = 512
DOCS = 4
N_BLK = 4


def draw_queries(key, part):
    total_count = N_BLK * BLOCK_TOKENS
    query_group = QUERY_HEADS // KEY_VALUE_HEADS
    fresh_state = jax.random.fold_in(key, 11)
    base_offset = jnp.clip(jax.random.normal(fresh_state, (total_count, KEY_VALUE_HEADS, query_group, HEAD_WIDTH), jnp.float32), -4.5, 4.5)
    return base_offset.reshape(N_BLK, BLOCK_TOKENS, QUERY_HEADS * HEAD_WIDTH).astype(jnp.bfloat16)


def draw_keys(key, part):
    total_count = N_BLK * BLOCK_TOKENS
    fresh_state = jax.random.fold_in(key, 13)
    base_offset = jnp.clip(jax.random.normal(fresh_state, (total_count, KEY_VALUE_HEADS, HEAD_WIDTH), jnp.float32), -4.5, 4.5)
    return base_offset.reshape(N_BLK, BLOCK_TOKENS, KEY_VALUE_HEADS * HEAD_WIDTH).astype(jnp.bfloat16)


def block_scale(own_key, dims, cuts, smallest, top_value):
    level, own = 1.0, jax.random.fold_in(own_key, 6)
    for dim, shards_of in cuts:
        steps = jnp.exp(jax.random.uniform(jax.random.fold_in(own, dim), (shards_of,), jnp.float32, smallest / len(cuts), top_value / len(cuts)))
        level = level * jnp.repeat(steps, dims[dim] // shards_of).reshape([-1 if axis == dim else 1 for axis in range(len(dims))])
    return level


def length_profile(amount, total, limit, lean):
    weights = [(1 << 20) // math.isqrt(grade ** lean) + 1 for grade in range(2, amount + 1)]
    spare, counts = total - limit - (amount - 1), [1] * (amount - 1)
    while spare > 0:
        candidates = [i for i in range(amount - 1) if counts[i] < limit]
        pool, left = sum([weights[i] for i in candidates]), spare
        for i in candidates:
            extra = min(limit - counts[i], max(1, left * weights[i] // pool), spare)
            counts[i] = counts[i] + extra
            spare = spare - extra
    return np.array([limit] + counts)


def uneven_parts(own_key, amount, total, limit, skew):
    if amount == 2:
        one = jax.random.randint(own_key, (), max(1, total - limit), min(limit, total - 1) + 1)
        return jnp.stack([one, total - one])
    lengths = jnp.asarray(length_profile(amount, total, limit, skew), jnp.int32)
    twos = (amount - 1) // 2
    donor, receiver = lengths[1:1 + 2 * twos:2], lengths[2:2 + 2 * twos:2]
    margin = jnp.minimum(donor - 1, limit - receiver)
    shifted = jax.random.randint(jax.random.fold_in(own_key, 1), (twos,), 0, 1 << 20) % (margin + 1)
    lengths = lengths.at[1:1 + 2 * twos:2].set(donor - shifted).at[2:2 + 2 * twos:2].set(receiver + shifted)
    return lengths[jax.random.permutation(jax.random.fold_in(own_key, 2), amount)]


def gaussian(own_key, dims, scale, reach, cuts=(), kind=jnp.bfloat16):
    values = jax.random.normal(own_key, dims, jnp.float32) * scale
    if len(cuts) > 0:
        values = block_scale(own_key, dims, cuts, -0.22, 0.18) * values
    return jnp.clip(values, min=-reach, max=reach).astype(kind)


def setup_inputs(seed: int = 0, part: int = 0) -> dict:
    seeds = jax.random.split(jax.random.key(seed), 5)
    part_keys = jax.random.split(jax.random.fold_in(seeds[4], part), 5)
    return {
        "queries": draw_queries(jax.random.fold_in(jax.random.fold_in(seeds[4], part), 71), part),
        "keys": draw_keys(jax.random.fold_in(jax.random.fold_in(seeds[4], part), 71), part),
        "values": gaussian(part_keys[2], (N_BLK, BLOCK_TOKENS, KEY_VALUE_HEADS * HEAD_WIDTH), 1.0, 6.0, ((0, 4), (1, 8))),
        "doc_blocks": uneven_parts(part_keys[3], DOCS, N_BLK * BLOCK_TOKENS // BLOCK, (N_BLK // 2 + 1) * BLOCK_TOKENS // BLOCK, 2).astype(jnp.int32),
    }


def reference(queries, keys, values, doc_blocks):
    total_count = N_BLK * BLOCK_TOKENS
    query_group = QUERY_HEADS // KEY_VALUE_HEADS
    scale = HEAD_WIDTH ** -0.5
    q = queries.reshape(N_BLK, BLOCK_TOKENS, KEY_VALUE_HEADS, query_group, HEAD_WIDTH)
    key_rows = keys.reshape(N_BLK, BLOCK_TOKENS, KEY_VALUE_HEADS, HEAD_WIDTH)
    value_rows = values.reshape(N_BLK, BLOCK_TOKENS, KEY_VALUE_HEADS, HEAD_WIDTH)
    ends = jnp.cumsum(doc_blocks).astype(jnp.int32) * BLOCK
    pos = jnp.arange(total_count, dtype=jnp.int32)
    seg = jnp.sum((pos[:, None] >= ends[None, :]).astype(jnp.int32), axis=1).astype(jnp.int32)
    seg = seg.reshape(N_BLK, BLOCK_TOKENS)
    first_seg = seg[:, 0]
    last_seg = seg[:, -1]

    def one_slot(index):
        qs = lax.dynamic_index_in_dim(q, index, 0, keepdims=False).astype(jnp.float32)
        qseg = lax.dynamic_index_in_dim(seg, index, 0, keepdims=False)
        qpos = index * BLOCK_TOKENS + jnp.arange(BLOCK_TOKENS, dtype=jnp.int32)
        qfirst = lax.dynamic_index_in_dim(first_seg, index, 0, keepdims=False)

        def scores_of(other):
            ks = lax.dynamic_index_in_dim(key_rows, other, 0, keepdims=False).astype(jnp.float32)
            kseg = lax.dynamic_index_in_dim(seg, other, 0, keepdims=False)
            kpos = other * BLOCK_TOKENS + jnp.arange(BLOCK_TOKENS, dtype=jnp.int32)
            allowed = (qseg[:, None] == kseg[None, :]) & (kpos[None, :] <= qpos[:, None])
            scores = jnp.einsum('tghd,sgd->ghts', qs, ks) * scale
            return allowed, jnp.where(allowed[None, None], scores, -1e30)

        def useful(other):
            klast = lax.dynamic_index_in_dim(last_seg, other, 0, keepdims=False)
            return (other <= index) & (klast >= qfirst)

        def max_step(most, other):
            def work(current):
                return jnp.maximum(current, jnp.max(scores_of(other)[1], axis=-1))
            return lax.cond(useful(other), work, lambda current: current, most), None

        start_most = jnp.full((KEY_VALUE_HEADS, query_group, BLOCK_TOKENS), -1e30, jnp.float32)
        most, unused = lax.scan(max_step, start_most, jnp.arange(N_BLK, dtype=jnp.int32))

        def sum_step(carry, other):
            def work(state):
                total, accum = state
                allowed, scores = scores_of(other)
                expo = jnp.where(allowed[None, None], jnp.exp(scores - most[..., None]), 0.0)
                weights = expo.astype(jnp.bfloat16).astype(jnp.float32)
                vs = lax.dynamic_index_in_dim(value_rows, other, 0, keepdims=False).astype(jnp.float32)
                return total + jnp.sum(expo, axis=-1), accum + jnp.einsum('ghts,sgd->ghtd', weights, vs)
            return lax.cond(useful(other), work, lambda state: state, carry), None

        start_state = (jnp.zeros((KEY_VALUE_HEADS, query_group, BLOCK_TOKENS), jnp.float32), jnp.zeros((KEY_VALUE_HEADS, query_group, BLOCK_TOKENS, HEAD_WIDTH), jnp.float32))
        (total, accum), unused = lax.scan(sum_step, start_state, jnp.arange(N_BLK, dtype=jnp.int32))
        out = (accum / total[..., None]).astype(jnp.bfloat16)
        return jnp.transpose(out, (2, 0, 1, 3)).reshape(BLOCK_TOKENS, QUERY_HEADS * HEAD_WIDTH)

    return lax.map(one_slot, jnp.arange(N_BLK, dtype=jnp.int32))
```

```python
import functools
import math

import jax
import jax.numpy as jnp
from jax import lax
from jax.experimental import pallas as pl
from jax.experimental.pallas import tpu as pltpu
from jax.sharding import PartitionSpec as P

HEAD_WIDTH = 128
BLOCK = 128
FAR = 1e30
RATE = math.log2(math.e) / math.sqrt(HEAD_WIDTH)


def segment_of(positions, ends):
    return jnp.sum((positions[:, None] >= ends[None, :]).astype(jnp.int32), axis=1)


def general(queries, keys, values, doc_blocks):
    moved_q, moved_k, moved_v = (
        lax.all_to_all(queries, "uly", split_axis=2, concat_axis=1, tiled=True),
        lax.all_to_all(keys, "uly", split_axis=2, concat_axis=1, tiled=True),
        lax.all_to_all(values, "uly", split_axis=2, concat_axis=1, tiled=True),
    )
    slot = moved_q.shape[1]
    local_q = moved_q.shape[2] // HEAD_WIDTH
    local_kv = moved_k.shape[2] // HEAD_WIDTH
    query_group = local_q // local_kv
    scale = HEAD_WIDTH ** (-0.5)
    first_index = lax.axis_index("blk") * slot
    ends = jnp.cumsum(doc_blocks) * BLOCK
    qpos = first_index + jnp.arange(slot, dtype=jnp.int32)
    qseg = segment_of(qpos, ends)
    qheads = jnp.transpose(moved_q[0].reshape(slot, local_q, HEAD_WIDTH), (1, 0, 2))
    stacked = jnp.concatenate([moved_k, moved_v], axis=0)

    def allowed_for(kpos):
        kseg = segment_of(kpos, ends)
        return (qseg[:, None] == kseg[None, :]) & (kpos[None, :] <= qpos[:, None])

    start_state = (
        jnp.full((local_q, slot), -1e30, jnp.float32),
        jnp.zeros((local_q, slot), jnp.float32),
        jnp.zeros((local_q, slot, HEAD_WIDTH), jnp.float32),
    )
    piece = lax.all_gather(stacked, "blk", axis=1, tiled=True)
    start = jnp.int32(0)
    count = piece.shape[1]

    def work(state):
        key_piece = piece[0].reshape(count, local_kv, HEAD_WIDTH)
        value_piece = piece[1].reshape(count, local_kv, HEAD_WIDTH)
        allowed = allowed_for(jnp.arange(count, dtype=jnp.int32))

        def one_head(inputs):
            head, running, summed, accum = inputs
            qh = lax.dynamic_index_in_dim(qheads, head, 0, keepdims=False)
            kh = lax.dynamic_index_in_dim(key_piece, head // query_group, 1, keepdims=False)
            vh = lax.dynamic_index_in_dim(value_piece, head // query_group, 1, keepdims=False)
            scores = jnp.dot(qh, kh.T, preferred_element_type=jnp.float32) * scale
            scores = jnp.where(allowed, scores, -1e30)
            newest = jnp.maximum(running, jnp.max(scores, axis=1))
            expo = jnp.where(allowed, jnp.exp(scores - newest[:, None]), 0.0)
            factor = jnp.exp(running - newest)
            summed = summed * factor + jnp.sum(expo, axis=1)
            accum = accum * factor[:, None] + jnp.dot(
                expo.astype(jnp.bfloat16), vh, preferred_element_type=jnp.float32
            )
            return (newest, summed, accum)

        return lax.map(one_head, (jnp.arange(local_q, dtype=jnp.int32),) + tuple(state))

    last_seg = jnp.sum((start + count - 1 >= ends).astype(jnp.int32))
    useful = (start < first_index + slot) & (last_seg >= qseg[0])
    running, summed, accum = lax.cond(useful, work, lambda state: state, start_state)
    heads = (accum / summed[:, :, None]).astype(jnp.bfloat16)
    outputs = jnp.transpose(heads, (1, 0, 2)).reshape(1, slot, local_q * HEAD_WIDTH)
    return lax.all_to_all(outputs, "uly", split_axis=1, concat_axis=2, tiled=True)


def segment_starts(doc_blocks, positions):
    ends = jnp.cumsum(doc_blocks) * BLOCK
    return jnp.max(jnp.where(ends[None, :] <= positions[:, None], ends[None, :], 0), axis=1)


def spread(doc_blocks, slices, share, slot):
    first = lax.axis_index("uly") * share + jnp.arange(slices, dtype=jnp.int32) * slot
    return segment_starts(doc_blocks, first)


def update(q_ref, kv_ref, starts_ref, most, total, accum, g, other, me, dims, first):
    slices, share, group, kv_heads, slot = dims
    width = HEAD_WIDTH
    for b in range(slices):
        rows = [
            q_ref[b, :, pl.ds(pl.multiple_of((g * group + h) * width, width), width)]
            for h in range(group)
        ]
        q = jnp.concatenate(rows, axis=0)
        count = (b + 1) * share
        k = kv_ref[other, 0:count, pl.ds(pl.multiple_of(g * width, width), width)]
        v = kv_ref[other, 0:count, pl.ds(pl.multiple_of((kv_heads + g) * width, width), width)]
        scores = lax.dot_general(
            k, q, (((1,), (1,)), ((), ())), preferred_element_type=jnp.float32
        )
        start = starts_ref[b]
        parts, penalties, tops = [], [], []
        for c in range(b + 1):
            part = scores[c * share:(c + 1) * share]
            if first and c == b:
                token = lax.broadcasted_iota(jnp.int32, part.shape, 1) % share
                key = lax.broadcasted_iota(jnp.int32, part.shape, 0)
                part = jnp.where(key <= token, part, -FAR)
                penalty = jnp.float32(0)
            else:
                allowed = c * slot + other * share >= start
                if c == b:
                    allowed = allowed & (other < me)
                penalty = jnp.where(allowed, jnp.float32(0), jnp.float32(FAR))
            parts.append(part)
            penalties.append(penalty)
            tops.append(jnp.max(part, axis=0, keepdims=True) - penalty)
        top = functools.reduce(jnp.maximum, tops)
        if not first:
            old = most[g, b]
            top = jnp.maximum(top, old)
        scaled = top * RATE
        weights = [
            jnp.exp2(part * RATE - (scaled + penalty)) for part, penalty in zip(parts, penalties)
        ]
        summed = functools.reduce(
            jnp.add, [jnp.sum(weight, axis=0, keepdims=True) for weight in weights]
        )
        weights = jnp.concatenate([weight.astype(jnp.bfloat16) for weight in weights], axis=0)
        product = lax.dot_general(
            v, weights, (((0,), (0,)), ((), ())), preferred_element_type=jnp.float32
        )
        most[g, b] = top
        if first:
            total[g, b] = summed
            accum[g, b] = product
        else:
            factor = jnp.exp2((old - top) * RATE)
            total[g, b] = total[g, b] * factor + summed
            accum[g, b] = accum[g, b] * factor + product


def finish(out_ref, total, accum, g, dims):
    slices, share, group, kv_heads, slot = dims
    width = HEAD_WIDTH
    for b in range(slices):
        done = (accum[g, b] / total[g, b]).T.astype(jnp.bfloat16)
        for h in range(group):
            out_ref[b, :, pl.ds(pl.multiple_of((g * group + h) * width, width), width)] = done[
                h * share:(h + 1) * share
            ]


def attend(dims, n_uly, q_ref, kv_ref, starts_ref, out_ref, most, total, accum):
    me = lax.axis_index("uly")
    kv_heads = dims[3]

    @pl.loop(0, kv_heads)
    def _(g):
        update(q_ref, kv_ref, starts_ref, most, total, accum, g, me, me, dims, True)

        @pl.loop(1, n_uly)
        def _(step):
            other = lax.rem(me + step, n_uly)
            update(q_ref, kv_ref, starts_ref, most, total, accum, g, other, me, dims, False)

        finish(out_ref, total, accum, g, dims)


def by_heads(queries, keys, values, doc_blocks, n_uly, n_blk):
    share = queries.shape[1]
    slot = share * n_uly
    swap = lambda x: lax.all_to_all(x, "blk", split_axis=2, concat_axis=0, tiled=True)
    kv = jnp.concatenate([swap(keys), swap(values)], axis=2)
    kv = lax.all_gather(kv.reshape(n_blk * share, kv.shape[2]), "uly", axis=0)
    q = swap(queries)
    kv_heads = kv.shape[2] // (2 * HEAD_WIDTH)
    group = q.shape[2] // HEAD_WIDTH // kv_heads
    dims = (n_blk, share, group, kv_heads, slot)
    starts = spread(doc_blocks, n_blk, share, slot)
    vmem = pl.BlockSpec(memory_space=pltpu.VMEM)
    rows = group * share
    out = pl.pallas_call(
        functools.partial(attend, dims, n_uly),
        out_shape=jax.ShapeDtypeStruct(q.shape, jnp.bfloat16),
        in_specs=[vmem, vmem, pl.BlockSpec(memory_space=pltpu.SMEM)],
        out_specs=vmem,
        scratch_shapes=[
            pltpu.VMEM((kv_heads, n_blk, 1, rows), jnp.float32),
            pltpu.VMEM((kv_heads, n_blk, 1, rows), jnp.float32),
            pltpu.VMEM((kv_heads, n_blk, HEAD_WIDTH, rows), jnp.float32),
        ],
        compiler_params=pltpu.CompilerParams(vmem_limit_bytes=40 * 1024 * 1024),
    )(q, kv, starts)
    return lax.all_to_all(out, "blk", split_axis=0, concat_axis=2, tiled=True)


def solution(mesh):
    n_uly, n_blk = mesh.shape["uly"], mesh.shape["blk"]

    def on_device(queries, keys, values, doc_blocks):
        if (keys.shape[2] // HEAD_WIDTH) % n_blk == 0:
            return by_heads(queries, keys, values, doc_blocks, n_uly, n_blk)
        return general(queries, keys, values, doc_blocks)

    return jax.shard_map(
        on_device,
        mesh=mesh,
        in_specs=(
            P(("parts", "blk"), "uly", None),
            P(("parts", "blk"), "uly", None),
            P(("parts", "blk"), "uly", None),
            P("parts"),
        ),
        out_specs=P(("parts", "blk"), "uly", None),
        check_vma=False,
    )
```

```python
import functools
import math

import jax
import jax.numpy as jnp
from jax import lax
from jax.experimental import pallas as pl
from jax.experimental.pallas import tpu as pltpu
from jax.sharding import PartitionSpec as P

HEAD_WIDTH = 128
BLOCK = 128
FAR = 1e30
RATE = math.log2(math.e) / math.sqrt(HEAD_WIDTH)


def segment_of(positions, ends):
    return jnp.sum((positions[:, None] >= ends[None, :]).astype(jnp.int32), axis=1)


def general(queries, keys, values, doc_blocks):
    moved_q, moved_k, moved_v = (
        lax.all_to_all(queries, "uly", split_axis=2, concat_axis=1, tiled=True),
        lax.all_to_all(keys, "uly", split_axis=2, concat_axis=1, tiled=True),
        lax.all_to_all(values, "uly", split_axis=2, concat_axis=1, tiled=True),
    )
    slot = moved_q.shape[1]
    local_q = moved_q.shape[2] // HEAD_WIDTH
    local_kv = moved_k.shape[2] // HEAD_WIDTH
    query_group = local_q // local_kv
    scale = HEAD_WIDTH ** (-0.5)
    first_index = lax.axis_index("blk") * slot
    ends = jnp.cumsum(doc_blocks) * BLOCK
    qpos = first_index + jnp.arange(slot, dtype=jnp.int32)
    qseg = segment_of(qpos, ends)
    qheads = jnp.transpose(moved_q[0].reshape(slot, local_q, HEAD_WIDTH), (1, 0, 2))
    stacked = jnp.concatenate([moved_k, moved_v], axis=0)

    def allowed_for(kpos):
        kseg = segment_of(kpos, ends)
        return (qseg[:, None] == kseg[None, :]) & (kpos[None, :] <= qpos[:, None])

    start_state = (
        jnp.full((local_q, slot), -1e30, jnp.float32),
        jnp.zeros((local_q, slot), jnp.float32),
        jnp.zeros((local_q, slot, HEAD_WIDTH), jnp.float32),
    )
    piece = lax.all_gather(stacked, "blk", axis=1, tiled=True)
    start = jnp.int32(0)
    count = piece.shape[1]

    def work(state):
        key_piece = piece[0].reshape(count, local_kv, HEAD_WIDTH)
        value_piece = piece[1].reshape(count, local_kv, HEAD_WIDTH)
        allowed = allowed_for(jnp.arange(count, dtype=jnp.int32))

        def one_head(inputs):
            head, running, summed, accum = inputs
            qh = lax.dynamic_index_in_dim(qheads, head, 0, keepdims=False)
            kh = lax.dynamic_index_in_dim(key_piece, head // query_group, 1, keepdims=False)
            vh = lax.dynamic_index_in_dim(value_piece, head // query_group, 1, keepdims=False)
            scores = jnp.dot(qh, kh.T, preferred_element_type=jnp.float32) * scale
            scores = jnp.where(allowed, scores, -1e30)
            newest = jnp.maximum(running, jnp.max(scores, axis=1))
            expo = jnp.where(allowed, jnp.exp(scores - newest[:, None]), 0.0)
            factor = jnp.exp(running - newest)
            summed = summed * factor + jnp.sum(expo, axis=1)
            accum = accum * factor[:, None] + jnp.dot(
                expo.astype(jnp.bfloat16), vh, preferred_element_type=jnp.float32
            )
            return (newest, summed, accum)

        return lax.map(one_head, (jnp.arange(local_q, dtype=jnp.int32),) + tuple(state))

    last_seg = jnp.sum((start + count - 1 >= ends).astype(jnp.int32))
    useful = (start < first_index + slot) & (last_seg >= qseg[0])
    running, summed, accum = lax.cond(useful, work, lambda state: state, start_state)
    heads = (accum / summed[:, :, None]).astype(jnp.bfloat16)
    outputs = jnp.transpose(heads, (1, 0, 2)).reshape(1, slot, local_q * HEAD_WIDTH)
    return lax.all_to_all(outputs, "uly", split_axis=1, concat_axis=2, tiled=True)


MESH = pl.DeviceIdType.MESH


def ring_place(device, columns):
    row, side = device // 2, device % 2
    return side * (2 * columns - 1 - row) + (1 - side) * row


def ring_device(place, columns):
    back = place // columns
    return back * ((2 * columns - 1 - place) * 2 + 1) + (1 - back) * (place * 2)


def update(q_buf, kv_buf, starts, state, g, others, me, dims, blocks, first):
    slices, share, group, slot = dims
    most, total, accum = state
    for b in blocks:
        q = jnp.concatenate(
            [q_buf[g, b, :, h * HEAD_WIDTH:(h + 1) * HEAD_WIDTH] for h in range(group)], axis=0
        )
        count = (b + 1) * share
        parts, penalties, tops = [], [], []
        for other in others:
            scores = lax.dot_general(
                kv_buf[0, g, other, 0:count, :], q, (((1,), (1,)), ((), ())),
                preferred_element_type=jnp.float32,
            )
            for c in range(b + 1):
                part = scores[c * share:(c + 1) * share]
                if first and c == b:
                    token = lax.broadcasted_iota(jnp.int32, part.shape, 1) % share
                    key = lax.broadcasted_iota(jnp.int32, part.shape, 0)
                    part = jnp.where(key <= token, part, -FAR)
                    penalty = jnp.float32(0)
                else:
                    allowed = c * slot + other * share >= starts[b]
                    if c == b:
                        allowed = jnp.logical_and(allowed, other < me)
                    penalty = jnp.where(allowed, jnp.float32(0), jnp.float32(FAR))
                parts.append(part)
                penalties.append(penalty)
                tops.append(jnp.max(part, axis=0, keepdims=True) - penalty)
        top = functools.reduce(jnp.maximum, tops)
        if not first:
            old = most[g, b]
            top = jnp.maximum(top, old)
        scaled = top * RATE
        weights = [
            jnp.exp2(part * RATE - (scaled + penalty)) for part, penalty in zip(parts, penalties)
        ]
        summed = jnp.sum(functools.reduce(jnp.add, weights), axis=0, keepdims=True)
        weights = [weight.astype(jnp.bfloat16) for weight in weights]
        products = [
            lax.dot_general(
                kv_buf[1, g, other, 0:count, :],
                jnp.concatenate(weights[i * (b + 1):(i + 1) * (b + 1)], axis=0),
                (((0,), (0,)), ((), ())), preferred_element_type=jnp.float32,
            )
            for i, other in enumerate(others)
        ]
        product = functools.reduce(jnp.add, products)
        most[g, b] = top
        if first:
            total[g, b] = summed
            accum[g, b] = product
        else:
            factor = jnp.exp2((old - top) * RATE)
            total[g, b] = total[g, b] * factor + summed
            accum[g, b] = accum[g, b] * factor + product


def attend(
    dims, n_uly, kv_heads, docs, q_ref, k_ref, v_ref, docs_ref, out_ref,
    q_buf, kv_buf, o_buf, most, total, accum,
    swap_send, swap_recv, q_send, q_recv, ring_send, ring_recv, o_send, o_recv,
):
    slices, share, group, slot = dims
    width = HEAD_WIDTH
    half = n_uly // 2
    me, block = lax.axis_index("uly"), lax.axis_index("blk")
    place = ring_place(me, half)
    at = lambda offset: ring_device(lax.rem(place + offset + n_uly, n_uly), half)
    ahead, behind = at(1), at(-1)
    state = (most, total, accum)
    wide = group * width

    barrier = pltpu.get_barrier_semaphore()
    for other in (ahead, behind):
        pl.semaphore_signal(barrier, inc=1, device_id={"uly": other}, device_id_type=MESH)
    for d in range(1, slices):
        peer = lax.rem(block + d, slices)
        pl.semaphore_signal(barrier, inc=1, device_id={"blk": peer}, device_id_type=MESH)
    pl.semaphore_wait(barrier, slices + 1)

    def rows(b):
        return pl.ds(pl.multiple_of(b * share, share), share)

    def columns(start, size):
        return pl.ds(pl.multiple_of(start, width), size)

    def swap_copy(part, g, d):
        peer = lax.rem(block + d, slices)
        return pltpu.make_async_remote_copy(
            src_ref=(k_ref, v_ref)[part].at[:, columns((peer * kv_heads + g) * width, width)],
            dst_ref=kv_buf.at[part, g, me, rows(block), :],
            send_sem=swap_send.at[part, g, d - 1],
            recv_sem=swap_recv.at[part, g, d - 1],
            device_id={"blk": peer},
            device_id_type=MESH,
        )

    def q_copy(g, d):
        peer = lax.rem(block + d, slices)
        return pltpu.make_async_remote_copy(
            src_ref=q_ref.at[:, columns((peer * kv_heads + g) * wide, wide)],
            dst_ref=q_buf.at[g, block],
            send_sem=q_send.at[g, d - 1],
            recv_sem=q_recv.at[g, d - 1],
            device_id={"blk": peer},
            device_id_type=MESH,
        )

    def o_copy(g, d):
        peer = lax.rem(block + d, slices)
        return pltpu.make_async_remote_copy(
            src_ref=o_buf.at[g, peer],
            dst_ref=out_ref.at[:, columns((block * kv_heads + g) * wide, wide)],
            send_sem=o_send.at[g, d - 1],
            recv_sem=o_recv.at[g, d - 1],
            device_id={"blk": peer},
            device_id_type=MESH,
        )

    def ring_copy(part, way, g, hop):
        origin = at(-hop) if way == 0 else at(hop)
        tile = kv_buf.at[part, g, origin]
        return pltpu.make_async_remote_copy(
            src_ref=tile,
            dst_ref=tile,
            send_sem=ring_send.at[part, way, g, hop],
            recv_sem=ring_recv.at[part, way, g, hop],
            device_id={"uly": ahead if way == 0 else behind},
            device_id_type=MESH,
        )

    def swap_wait(part, g):
        for d in range(1, slices):
            swap_copy(part, g, d).wait_recv()

    def hops(way, g):
        return half if way == g % 2 else half - 1

    def poll(part, g, s):
        if s == half - 2 and g + 1 < kv_heads:
            swap_wait(part, g + 1)
        for way in range(2):
            if s > hops(way, g):
                continue
            ring_copy(part, way, g, s - 1).wait_recv()
            if s < hops(way, g):
                ring_copy(part, way, g, s).start()
            if s == hops(way, g) - 1 and g + 1 < kv_heads:
                ring_copy(part, way, g + 1, 0).start()

    for g in range(kv_heads):
        for part in range(2):
            for d in range(1, slices):
                swap_copy(part, g, d).start()
        for d in range(1, slices):
            q_copy(g, d).start()
    for g in range(kv_heads):
        for part in range(2):
            kv_buf[part, g, me, rows(block), :] = (k_ref, v_ref)[part][
                :, columns((block * kv_heads + g) * width, width)
            ]
        q_buf[g, block] = q_ref[:, columns((block * kv_heads + g) * wide, wide)]
    for part in range(2):
        swap_wait(part, 0)
        for way in range(2):
            ring_copy(part, way, 0, 0).start()

    ends, so_far = [], 0
    for d in range(docs):
        so_far = so_far + docs_ref[d] * BLOCK
        ends.append(so_far)
    starts = []
    for b in range(slices):
        position = b * slot + me * share
        start = jnp.int32(0)
        for end in ends:
            start = jnp.where(end <= position, end, start)
        starts.append(start)

    every = range(slices)
    early, late = [b for b in every if b % 4 in (0, 3)], [b for b in every if b % 4 in (1, 2)]
    poll(0, 0, 1)
    poll(1, 0, 1)
    for g in range(kv_heads):
        for d in range(1, slices):
            q_copy(g, d).wait_recv()
        update(q_buf, kv_buf, starts, state, g, [me], me, dims, every, True)
        for s in range(1, half + 1):
            if s < half:
                others = [at(-s), at(s)]
            else:
                others = [at(half)]
            after = (g, s + 1) if s < half else (g + 1, 1)
            update(q_buf, kv_buf, starts, state, g, others, me, dims, early, False)
            if after[0] < kv_heads:
                poll(0, *after)
            update(q_buf, kv_buf, starts, state, g, others, me, dims, late, False)
            if after[0] < kv_heads:
                poll(1, *after)
        for b in every:
            done = (accum[g, b] / total[g, b]).T.astype(jnp.bfloat16)
            for h in range(group):
                o_buf[g, b, :, h * width:(h + 1) * width] = done[h * share:(h + 1) * share]
        for d in range(1, slices):
            o_copy(g, d).start()
        out_ref[:, columns((block * kv_heads + g) * wide, wide)] = o_buf[g, block]
    for g in range(kv_heads):
        for d in range(1, slices):
            for part in range(2):
                swap_copy(part, g, d).wait_send()
            q_copy(g, d).wait_send()
        for part in range(2):
            for way in range(2):
                for hop in range(hops(way, g)):
                    ring_copy(part, way, g, hop).wait_send()
        for d in range(1, slices):
            o_copy(g, d).wait()


def by_heads(queries, keys, values, doc_blocks, n_uly, n_blk):
    share = queries.shape[1]
    slot = share * n_uly
    kv_heads = keys.shape[2] // HEAD_WIDTH // n_blk
    group = queries.shape[2] // keys.shape[2]
    docs = doc_blocks.shape[0]
    dims = (n_blk, share, group, slot)
    vmem = pl.BlockSpec(memory_space=pltpu.VMEM)
    rows, wide, half = group * share, group * HEAD_WIDTH, n_uly // 2
    dma = pltpu.SemaphoreType.DMA
    out = pl.pallas_call(
        functools.partial(attend, dims, n_uly, kv_heads, docs),
        out_shape=jax.ShapeDtypeStruct(queries.shape[1:], jnp.bfloat16),
        in_specs=[vmem, vmem, vmem, pl.BlockSpec(memory_space=pltpu.SMEM)],
        out_specs=vmem,
        scratch_shapes=[
            pltpu.VMEM((kv_heads, n_blk, share, wide), jnp.bfloat16),
            pltpu.VMEM((2, kv_heads, n_uly, n_blk * share, HEAD_WIDTH), jnp.bfloat16),
            pltpu.VMEM((kv_heads, n_blk, share, wide), jnp.bfloat16),
            pltpu.VMEM((kv_heads, n_blk, 1, rows), jnp.float32),
            pltpu.VMEM((kv_heads, n_blk, 1, rows), jnp.float32),
            pltpu.VMEM((kv_heads, n_blk, HEAD_WIDTH, rows), jnp.float32),
            dma((2, kv_heads, n_blk - 1)),
            dma((2, kv_heads, n_blk - 1)),
            dma((kv_heads, n_blk - 1)),
            dma((kv_heads, n_blk - 1)),
            dma((2, 2, kv_heads, half)),
            dma((2, 2, kv_heads, half)),
            dma((kv_heads, n_blk - 1)),
            dma((kv_heads, n_blk - 1)),
        ],
        compiler_params=pltpu.CompilerParams(
            collective_id=0, has_side_effects=True, vmem_limit_bytes=48 * 1024 * 1024
        ),
    )(queries[0], keys[0], values[0], doc_blocks)
    return out[None]


def solution(mesh):
    n_uly, n_blk = mesh.shape["uly"], mesh.shape["blk"]

    def on_device(queries, keys, values, doc_blocks):
        if (keys.shape[2] // HEAD_WIDTH) % n_blk == 0 and n_uly % 2 == 0 and n_uly > 4:
            return by_heads(queries, keys, values, doc_blocks, n_uly, n_blk)
        return general(queries, keys, values, doc_blocks)

    return jax.shard_map(
        on_device,
        mesh=mesh,
        in_specs=(
            P(("parts", "blk"), "uly", None),
            P(("parts", "blk"), "uly", None),
            P(("parts", "blk"), "uly", None),
            P("parts"),
        ),
        out_specs=P(("parts", "blk"), "uly", None),
        check_vma=False,
    )
```

```python
import functools
import math

import jax
import jax.numpy as jnp
from jax import lax
from jax.experimental import pallas as pl
from jax.experimental.pallas import tpu as pltpu
from jax.sharding import PartitionSpec as P

HEAD_WIDTH = 128
BLOCK = 128
FAR = 1e30
RATE = math.log2(math.e) / math.sqrt(HEAD_WIDTH)


def segment_of(positions, ends):
    return jnp.sum((positions[:, None] >= ends[None, :]).astype(jnp.int32), axis=1)


def general(queries, keys, values, doc_blocks):
    moved_q, moved_k, moved_v = (
        lax.all_to_all(queries, "uly", split_axis=2, concat_axis=1, tiled=True),
        lax.all_to_all(keys, "uly", split_axis=2, concat_axis=1, tiled=True),
        lax.all_to_all(values, "uly", split_axis=2, concat_axis=1, tiled=True),
    )
    slot = moved_q.shape[1]
    local_q = moved_q.shape[2] // HEAD_WIDTH
    local_kv = moved_k.shape[2] // HEAD_WIDTH
    query_group = local_q // local_kv
    scale = HEAD_WIDTH ** (-0.5)
    first_index = lax.axis_index("blk") * slot
    ends = jnp.cumsum(doc_blocks) * BLOCK
    qpos = first_index + jnp.arange(slot, dtype=jnp.int32)
    qseg = segment_of(qpos, ends)
    qheads = jnp.transpose(moved_q[0].reshape(slot, local_q, HEAD_WIDTH), (1, 0, 2))
    stacked = jnp.concatenate([moved_k, moved_v], axis=0)

    def allowed_for(kpos):
        kseg = segment_of(kpos, ends)
        return (qseg[:, None] == kseg[None, :]) & (kpos[None, :] <= qpos[:, None])

    start_state = (
        jnp.full((local_q, slot), -1e30, jnp.float32),
        jnp.zeros((local_q, slot), jnp.float32),
        jnp.zeros((local_q, slot, HEAD_WIDTH), jnp.float32),
    )
    piece = lax.all_gather(stacked, "blk", axis=1, tiled=True)
    start = jnp.int32(0)
    count = piece.shape[1]

    def work(state):
        key_piece = piece[0].reshape(count, local_kv, HEAD_WIDTH)
        value_piece = piece[1].reshape(count, local_kv, HEAD_WIDTH)
        allowed = allowed_for(jnp.arange(count, dtype=jnp.int32))

        def one_head(inputs):
            head, running, summed, accum = inputs
            qh = lax.dynamic_index_in_dim(qheads, head, 0, keepdims=False)
            kh = lax.dynamic_index_in_dim(key_piece, head // query_group, 1, keepdims=False)
            vh = lax.dynamic_index_in_dim(value_piece, head // query_group, 1, keepdims=False)
            scores = jnp.dot(qh, kh.T, preferred_element_type=jnp.float32) * scale
            scores = jnp.where(allowed, scores, -1e30)
            newest = jnp.maximum(running, jnp.max(scores, axis=1))
            expo = jnp.where(allowed, jnp.exp(scores - newest[:, None]), 0.0)
            factor = jnp.exp(running - newest)
            summed = summed * factor + jnp.sum(expo, axis=1)
            accum = accum * factor[:, None] + jnp.dot(
                expo.astype(jnp.bfloat16), vh, preferred_element_type=jnp.float32
            )
            return (newest, summed, accum)

        return lax.map(one_head, (jnp.arange(local_q, dtype=jnp.int32),) + tuple(state))

    last_seg = jnp.sum((start + count - 1 >= ends).astype(jnp.int32))
    useful = (start < first_index + slot) & (last_seg >= qseg[0])
    running, summed, accum = lax.cond(useful, work, lambda state: state, start_state)
    heads = (accum / summed[:, :, None]).astype(jnp.bfloat16)
    outputs = jnp.transpose(heads, (1, 0, 2)).reshape(1, slot, local_q * HEAD_WIDTH)
    return lax.all_to_all(outputs, "uly", split_axis=1, concat_axis=2, tiled=True)


MESH = pl.DeviceIdType.MESH


def ring_place(device, columns):
    row, side = device // 2, device % 2
    return side * (2 * columns - 1 - row) + (1 - side) * row


def ring_device(place, columns):
    back = place // columns
    return back * ((2 * columns - 1 - place) * 2 + 1) + (1 - back) * (place * 2)


def update(q_buf, kv_buf, starts, state, g, others, me, dims, blocks, first):
    slices, share, group, slot = dims
    most, total, accum = state
    for b in blocks:
        q = jnp.concatenate(
            [q_buf[g, b, :, h * HEAD_WIDTH:(h + 1) * HEAD_WIDTH] for h in range(group)], axis=0
        )
        count = (b + 1) * share
        while count * len(others) % HEAD_WIDTH:
            count += share
        k = jnp.concatenate([kv_buf[0, g, other, 0:count, :] for other in others], axis=0)
        v = jnp.concatenate([kv_buf[1, g, other, 0:count, :] for other in others], axis=0)
        scores = lax.dot_general(
            q, k, (((1,), (1,)), ((), ())), preferred_element_type=jnp.float32
        )
        size = k.shape[0]
        token = b * slot + me * share
        lane = lax.broadcasted_iota(jnp.int32, (1, size), 1)
        index = lane % count
        origin = jnp.where(lane < count, others[0], others[-1])
        key = (index // share) * slot + index % share + origin * share
        allowed = key >= starts[b]
        if first:
            row = lax.broadcasted_iota(jnp.int32, scores.shape, 0) % share
            scores = jnp.where(jnp.logical_and(allowed, key <= token + row), scores, -FAR)
        else:
            allowed = jnp.logical_and(allowed, key < token)
            scores = scores + jnp.where(allowed, jnp.float32(0), jnp.float32(-FAR))
        tiles = [scores[:, i:i + HEAD_WIDTH] for i in range(0, size, HEAD_WIDTH)]
        top = jnp.max(functools.reduce(jnp.maximum, tiles), axis=1, keepdims=True)
        top = jnp.broadcast_to(top, (scores.shape[0], HEAD_WIDTH))
        if not first:
            old = most[g, b]
            top = jnp.maximum(top, old)
        weights = [jnp.exp2((tile - top) * RATE) for tile in tiles]
        summed = functools.reduce(jnp.add, weights)
        weights = jnp.concatenate([weight.astype(jnp.bfloat16) for weight in weights], axis=1)
        product = jnp.dot(weights, v, preferred_element_type=jnp.float32)
        most[g, b] = top
        if first:
            total[g, b] = summed
            accum[g, b] = product
        else:
            factor = jnp.exp2((old - top) * RATE)
            total[g, b] = total[g, b] * factor + summed
            accum[g, b] = accum[g, b] * factor + product


def attend(
    dims, n_uly, kv_heads, docs, q_ref, k_ref, v_ref, docs_ref, out_ref,
    q_buf, kv_buf, o_buf, most, total, accum,
    swap_send, swap_recv, q_send, q_recv, ring_send, ring_recv, o_send, o_recv, own_kv, own_q,
):
    slices, share, group, slot = dims
    width = HEAD_WIDTH
    half = n_uly // 2
    me, block = lax.axis_index("uly"), lax.axis_index("blk")
    place = ring_place(me, half)
    at = lambda offset: ring_device(lax.rem(place + offset + n_uly, n_uly), half)
    ahead, behind = at(1), at(-1)
    state = (most, total, accum)
    wide = group * width

    def rows(b):
        return pl.ds(pl.multiple_of(b * share, share), share)

    def columns(start, size):
        return pl.ds(pl.multiple_of(start, width), size)

    def own_kv_copy(part, g):
        return pltpu.make_async_copy(
            (k_ref, v_ref)[part].at[:, columns((block * kv_heads + g) * width, width)],
            kv_buf.at[part, g, me, rows(block), :],
            own_kv.at[part, g],
        )

    def own_q_copy(g):
        return pltpu.make_async_copy(
            q_ref.at[:, columns((block * kv_heads + g) * wide, wide)],
            q_buf.at[g, block],
            own_q.at[g],
        )

    for g in range(kv_heads):
        for part in range(2):
            own_kv_copy(part, g).start()
        own_q_copy(g).start()

    barrier = pltpu.get_barrier_semaphore()
    for other in (ahead, behind):
        pl.semaphore_signal(barrier, inc=1, device_id={"uly": other}, device_id_type=MESH)
    for d in range(1, slices):
        peer = lax.rem(block + d, slices)
        pl.semaphore_signal(barrier, inc=1, device_id={"blk": peer}, device_id_type=MESH)
    pl.semaphore_wait(barrier, slices + 1)

    def swap_copy(part, g, d):
        peer = lax.rem(block + d, slices)
        return pltpu.make_async_remote_copy(
            src_ref=(k_ref, v_ref)[part].at[:, columns((peer * kv_heads + g) * width, width)],
            dst_ref=kv_buf.at[part, g, me, rows(block), :],
            send_sem=swap_send.at[part, g, d - 1],
            recv_sem=swap_recv.at[part, g, d - 1],
            device_id={"blk": peer},
            device_id_type=MESH,
        )

    def q_copy(g, d):
        peer = lax.rem(block + d, slices)
        return pltpu.make_async_remote_copy(
            src_ref=q_ref.at[:, columns((peer * kv_heads + g) * wide, wide)],
            dst_ref=q_buf.at[g, block],
            send_sem=q_send.at[g, d - 1],
            recv_sem=q_recv.at[g, d - 1],
            device_id={"blk": peer},
            device_id_type=MESH,
        )

    def o_copy(g, peer):
        d = lax.rem(peer - block + slices, slices)
        return pltpu.make_async_remote_copy(
            src_ref=o_buf.at[g, peer],
            dst_ref=out_ref.at[:, columns((block * kv_heads + g) * wide, wide)],
            send_sem=o_send.at[g, d - 1],
            recv_sem=o_recv.at[g, d - 1],
            device_id={"blk": peer},
            device_id_type=MESH,
        )

    def ring_copy(part, way, g, hop):
        origin = at(-hop) if way == 0 else at(hop)
        tile = kv_buf.at[part, g, origin]
        return pltpu.make_async_remote_copy(
            src_ref=tile,
            dst_ref=tile,
            send_sem=ring_send.at[part, way, g, hop],
            recv_sem=ring_recv.at[part, way, g, hop],
            device_id={"uly": ahead if way == 0 else behind},
            device_id_type=MESH,
        )

    def swap_wait(part, g):
        own_kv_copy(part, g).wait()
        for d in range(1, slices):
            swap_copy(part, g, d).wait_recv()

    def hops(way, g):
        return half if way == g % 2 else half - 1

    def poll(part, g, s):
        if s == half - 2 and g + 1 < kv_heads:
            swap_wait(part, g + 1)
        for way in range(2):
            if s > hops(way, g):
                continue
            ring_copy(part, way, g, s - 1).wait_recv()
            if s < hops(way, g):
                ring_copy(part, way, g, s).start()
            if s == hops(way, g) - 1 and g + 1 < kv_heads:
                ring_copy(part, way, g + 1, 0).start()

    for g in range(kv_heads):
        for part in range(2):
            for d in range(1, slices):
                swap_copy(part, g, d).start()
        for d in range(1, slices):
            q_copy(g, d).start()
    for part in range(2):
        swap_wait(part, 0)
        for way in range(2):
            ring_copy(part, way, 0, 0).start()

    ends, so_far = [], 0
    for d in range(docs):
        so_far = so_far + docs_ref[d] * BLOCK
        ends.append(so_far)
    starts = []
    for b in range(slices):
        position = b * slot + me * share
        start = jnp.int32(0)
        for end in ends:
            start = jnp.where(end <= position, end, start)
        starts.append(start)

    every = range(slices)
    early, late = [b for b in every if b % 4 in (0, 3)], [b for b in every if b % 4 in (1, 2)]
    poll(0, 0, 1)
    poll(1, 0, 1)
    for g in range(kv_heads):
        for d in range(1, slices):
            q_copy(g, d).wait_recv()
        own_q_copy(g).wait()
        update(q_buf, kv_buf, starts, state, g, [me], me, dims, every, True)
        for s in range(1, half + 1):
            if s < half:
                others = [at(-s), at(s)]
            else:
                others = [at(half)]
            after = (g, s + 1) if s < half else (g + 1, 1)
            for part, blocks in enumerate((early, late)):
                for b in blocks:
                    update(q_buf, kv_buf, starts, state, g, others, me, dims, [b], False)
                    if s == half:
                        done = accum[g, b] / jnp.sum(total[g, b], axis=1, keepdims=True)
                        done = done.astype(jnp.bfloat16)
                        for h in range(group):
                            o_buf[g, b, :, h * width:(h + 1) * width] = done[
                                h * share:(h + 1) * share
                            ]
                        pl.when(b != block)(lambda b=b: o_copy(g, b).start())
                if after[0] < kv_heads:
                    poll(part, *after)
        out_ref[:, columns((block * kv_heads + g) * wide, wide)] = o_buf[g, block]
    for g in range(kv_heads):
        for d in range(1, slices):
            for part in range(2):
                swap_copy(part, g, d).wait_send()
            q_copy(g, d).wait_send()
        for part in range(2):
            for way in range(2):
                for hop in range(hops(way, g)):
                    ring_copy(part, way, g, hop).wait_send()
        for d in range(1, slices):
            o_copy(g, lax.rem(block + d, slices)).wait()


def by_heads(queries, keys, values, doc_blocks, n_uly, n_blk):
    share = queries.shape[1]
    slot = share * n_uly
    kv_heads = keys.shape[2] // HEAD_WIDTH // n_blk
    group = queries.shape[2] // keys.shape[2]
    docs = doc_blocks.shape[0]
    dims = (n_blk, share, group, slot)
    vmem = pl.BlockSpec(memory_space=pltpu.VMEM)
    anywhere = pl.BlockSpec(memory_space=pl.ANY)
    rows, wide, half = group * share, group * HEAD_WIDTH, n_uly // 2
    dma = pltpu.SemaphoreType.DMA
    out = pl.pallas_call(
        functools.partial(attend, dims, n_uly, kv_heads, docs),
        out_shape=jax.ShapeDtypeStruct(queries.shape[1:], jnp.bfloat16),
        in_specs=[anywhere, anywhere, anywhere, pl.BlockSpec(memory_space=pltpu.SMEM)],
        out_specs=vmem,
        scratch_shapes=[
            pltpu.VMEM((kv_heads, n_blk, share, wide), jnp.bfloat16),
            pltpu.VMEM((2, kv_heads, n_uly, n_blk * share, HEAD_WIDTH), jnp.bfloat16),
            pltpu.VMEM((kv_heads, n_blk, share, wide), jnp.bfloat16),
            pltpu.VMEM((kv_heads, n_blk, rows, HEAD_WIDTH), jnp.float32),
            pltpu.VMEM((kv_heads, n_blk, rows, HEAD_WIDTH), jnp.float32),
            pltpu.VMEM((kv_heads, n_blk, rows, HEAD_WIDTH), jnp.float32),
            dma((2, kv_heads, n_blk - 1)),
            dma((2, kv_heads, n_blk - 1)),
            dma((kv_heads, n_blk - 1)),
            dma((kv_heads, n_blk - 1)),
            dma((2, 2, kv_heads, half)),
            dma((2, 2, kv_heads, half)),
            dma((kv_heads, n_blk - 1)),
            dma((kv_heads, n_blk - 1)),
            dma((2, kv_heads)),
            dma((kv_heads,)),
        ],
        compiler_params=pltpu.CompilerParams(
            collective_id=0, has_side_effects=True, vmem_limit_bytes=60 * 1024 * 1024
        ),
    )(queries[0], keys[0], values[0], doc_blocks)
    return out[None]


def solution(mesh):
    n_uly, n_blk = mesh.shape["uly"], mesh.shape["blk"]

    def on_device(queries, keys, values, doc_blocks):
        if (keys.shape[2] // HEAD_WIDTH) % n_blk == 0 and n_uly % 2 == 0 and n_uly > 4:
            return by_heads(queries, keys, values, doc_blocks, n_uly, n_blk)
        return general(queries, keys, values, doc_blocks)

    return jax.shard_map(
        on_device,
        mesh=mesh,
        in_specs=(
            P(("parts", "blk"), "uly", None),
            P(("parts", "blk"), "uly", None),
            P(("parts", "blk"), "uly", None),
            P("parts"),
        ),
        out_specs=P(("parts", "blk"), "uly", None),
        check_vma=False,
    )
```

```python
import functools
import math

import jax
import jax.numpy as jnp
from jax import lax
from jax.experimental import pallas as pl
from jax.experimental.pallas import tpu as pltpu
from jax.sharding import PartitionSpec as P

HEAD_WIDTH = 128
BLOCK = 128
FAR = 1e30
RATE = math.log2(math.e) / math.sqrt(HEAD_WIDTH)


def segment_of(positions, ends):
    return jnp.sum((positions[:, None] >= ends[None, :]).astype(jnp.int32), axis=1)


def general(queries, keys, values, doc_blocks):
    moved_q, moved_k, moved_v = (
        lax.all_to_all(queries, "uly", split_axis=2, concat_axis=1, tiled=True),
        lax.all_to_all(keys, "uly", split_axis=2, concat_axis=1, tiled=True),
        lax.all_to_all(values, "uly", split_axis=2, concat_axis=1, tiled=True),
    )
    slot = moved_q.shape[1]
    local_q = moved_q.shape[2] // HEAD_WIDTH
    local_kv = moved_k.shape[2] // HEAD_WIDTH
    query_group = local_q // local_kv
    scale = HEAD_WIDTH ** (-0.5)
    first_index = lax.axis_index("blk") * slot
    ends = jnp.cumsum(doc_blocks) * BLOCK
    qpos = first_index + jnp.arange(slot, dtype=jnp.int32)
    qseg = segment_of(qpos, ends)
    qheads = jnp.transpose(moved_q[0].reshape(slot, local_q, HEAD_WIDTH), (1, 0, 2))
    stacked = jnp.concatenate([moved_k, moved_v], axis=0)

    def allowed_for(kpos):
        kseg = segment_of(kpos, ends)
        return (qseg[:, None] == kseg[None, :]) & (kpos[None, :] <= qpos[:, None])

    start_state = (
        jnp.full((local_q, slot), -1e30, jnp.float32),
        jnp.zeros((local_q, slot), jnp.float32),
        jnp.zeros((local_q, slot, HEAD_WIDTH), jnp.float32),
    )
    piece = lax.all_gather(stacked, "blk", axis=1, tiled=True)
    start = jnp.int32(0)
    count = piece.shape[1]

    def work(state):
        key_piece = piece[0].reshape(count, local_kv, HEAD_WIDTH)
        value_piece = piece[1].reshape(count, local_kv, HEAD_WIDTH)
        allowed = allowed_for(jnp.arange(count, dtype=jnp.int32))

        def one_head(inputs):
            head, running, summed, accum = inputs
            qh = lax.dynamic_index_in_dim(qheads, head, 0, keepdims=False)
            kh = lax.dynamic_index_in_dim(key_piece, head // query_group, 1, keepdims=False)
            vh = lax.dynamic_index_in_dim(value_piece, head // query_group, 1, keepdims=False)
            scores = jnp.dot(qh, kh.T, preferred_element_type=jnp.float32) * scale
            scores = jnp.where(allowed, scores, -1e30)
            newest = jnp.maximum(running, jnp.max(scores, axis=1))
            expo = jnp.where(allowed, jnp.exp(scores - newest[:, None]), 0.0)
            factor = jnp.exp(running - newest)
            summed = summed * factor + jnp.sum(expo, axis=1)
            accum = accum * factor[:, None] + jnp.dot(
                expo.astype(jnp.bfloat16), vh, preferred_element_type=jnp.float32
            )
            return (newest, summed, accum)

        return lax.map(one_head, (jnp.arange(local_q, dtype=jnp.int32),) + tuple(state))

    last_seg = jnp.sum((start + count - 1 >= ends).astype(jnp.int32))
    useful = (start < first_index + slot) & (last_seg >= qseg[0])
    running, summed, accum = lax.cond(useful, work, lambda state: state, start_state)
    heads = (accum / summed[:, :, None]).astype(jnp.bfloat16)
    outputs = jnp.transpose(heads, (1, 0, 2)).reshape(1, slot, local_q * HEAD_WIDTH)
    return lax.all_to_all(outputs, "uly", split_axis=1, concat_axis=2, tiled=True)


MESH = pl.DeviceIdType.MESH


def ring_place(device, columns):
    row, side = device // 2, device % 2
    return side * (2 * columns - 1 - row) + (1 - side) * row


def ring_device(place, columns):
    back = place // columns
    return back * ((2 * columns - 1 - place) * 2 + 1) + (1 - back) * (place * 2)


def update(q_buf, kv_buf, starts, state, g, others, me, dims, blocks, first):
    slices, share, group, slot = dims
    most, total, accum = state
    for b in blocks:
        q = jnp.concatenate(
            [q_buf[g, b, :, h * HEAD_WIDTH:(h + 1) * HEAD_WIDTH] for h in range(group)], axis=0
        )
        count = (b + 1) * share
        while count * len(others) % HEAD_WIDTH:
            count += share
        k = jnp.concatenate([kv_buf[0, g, other, 0:count, :] for other in others], axis=0)
        v = jnp.concatenate([kv_buf[1, g, other, 0:count, :] for other in others], axis=0)
        scores = lax.dot_general(
            q, k, (((1,), (1,)), ((), ())), preferred_element_type=jnp.float32
        )
        size = k.shape[0]
        token = b * slot + me * share
        lane = lax.broadcasted_iota(jnp.int32, (1, size), 1)
        index = lane % count
        origin = jnp.where(lane < count, others[0], others[-1])
        key = (index // share) * slot + index % share + origin * share
        allowed = key >= starts[b]
        if first:
            row = lax.broadcasted_iota(jnp.int32, scores.shape, 0) % share
            scores = jnp.where(jnp.logical_and(allowed, key <= token + row), scores, -FAR)
        else:
            allowed = jnp.logical_and(allowed, key < token)
            scores = scores + jnp.where(allowed, jnp.float32(0), jnp.float32(-FAR))
        tiles = [scores[:, i:i + HEAD_WIDTH] for i in range(0, size, HEAD_WIDTH)]
        top = jnp.max(functools.reduce(jnp.maximum, tiles), axis=1, keepdims=True)
        top = jnp.broadcast_to(top, (scores.shape[0], HEAD_WIDTH))
        if not first:
            old = most[g, b]
            top = jnp.maximum(top, old)
        weights = [jnp.exp2((tile - top) * RATE) for tile in tiles]
        summed = functools.reduce(jnp.add, weights)
        weights = jnp.concatenate([weight.astype(jnp.bfloat16) for weight in weights], axis=1)
        product = jnp.dot(weights, v, preferred_element_type=jnp.float32)
        most[g, b] = top
        if first:
            total[g, b] = summed
            accum[g, b] = product
        else:
            factor = jnp.exp2((old - top) * RATE)
            total[g, b] = total[g, b] * factor + summed
            accum[g, b] = accum[g, b] * factor + product


def attend(
    dims, n_uly, kv_heads, docs, q_ref, k_ref, v_ref, docs_ref, out_ref,
    q_buf, kv_buf, o_buf, most, total, accum,
    swap_send, swap_recv, q_send, q_recv, ring_send, ring_recv, o_send, o_recv, own_kv, own_q,
):
    slices, share, group, slot = dims
    width = HEAD_WIDTH
    half = n_uly // 2
    me, block = lax.axis_index("uly"), lax.axis_index("blk")
    place = ring_place(me, half)
    at = lambda offset: ring_device(lax.rem(place + offset + n_uly, n_uly), half)
    ahead, behind = at(1), at(-1)
    state = (most, total, accum)
    wide = group * width

    def rows(b):
        return pl.ds(pl.multiple_of(b * share, share), share)

    def columns(start, size):
        return pl.ds(pl.multiple_of(start, width), size)

    def own_kv_copy(part, g):
        return pltpu.make_async_copy(
            (k_ref, v_ref)[part].at[:, columns((block * kv_heads + g) * width, width)],
            kv_buf.at[part, g, me, rows(block), :],
            own_kv.at[part, g],
        )

    def own_q_copy(g):
        return pltpu.make_async_copy(
            q_ref.at[:, columns((block * kv_heads + g) * wide, wide)],
            q_buf.at[g, block],
            own_q.at[g],
        )

    for g in range(kv_heads):
        for part in range(2):
            own_kv_copy(part, g).start()
        own_q_copy(g).start()

    barrier = pltpu.get_barrier_semaphore()
    for other in (ahead, behind):
        pl.semaphore_signal(barrier, inc=1, device_id={"uly": other}, device_id_type=MESH)
    for d in range(1, slices):
        peer = lax.rem(block + d, slices)
        pl.semaphore_signal(barrier, inc=1, device_id={"blk": peer}, device_id_type=MESH)
    pl.semaphore_wait(barrier, slices + 1)

    def swap_copy(part, g, d):
        peer = lax.rem(block + d, slices)
        return pltpu.make_async_remote_copy(
            src_ref=(k_ref, v_ref)[part].at[:, columns((peer * kv_heads + g) * width, width)],
            dst_ref=kv_buf.at[part, g, me, rows(block), :],
            send_sem=swap_send.at[part, g, d - 1],
            recv_sem=swap_recv.at[part, g, d - 1],
            device_id={"blk": peer},
            device_id_type=MESH,
        )

    def q_copy(g, d):
        peer = lax.rem(block + d, slices)
        return pltpu.make_async_remote_copy(
            src_ref=q_ref.at[:, columns((peer * kv_heads + g) * wide, wide)],
            dst_ref=q_buf.at[g, block],
            send_sem=q_send.at[g, d - 1],
            recv_sem=q_recv.at[g, d - 1],
            device_id={"blk": peer},
            device_id_type=MESH,
        )

    def o_copy(g, peer):
        d = lax.rem(peer - block + slices, slices)
        return pltpu.make_async_remote_copy(
            src_ref=o_buf.at[g, peer],
            dst_ref=out_ref.at[:, columns((block * kv_heads + g) * wide, wide)],
            send_sem=o_send.at[g, d - 1],
            recv_sem=o_recv.at[g, d - 1],
            device_id={"blk": peer},
            device_id_type=MESH,
        )

    def ring_copy(part, way, g, hop):
        origin = at(-hop) if way == 0 else at(hop)
        tile = kv_buf.at[part, g, origin]
        return pltpu.make_async_remote_copy(
            src_ref=tile,
            dst_ref=tile,
            send_sem=ring_send.at[part, way, g, hop],
            recv_sem=ring_recv.at[part, way, g, hop],
            device_id={"uly": ahead if way == 0 else behind},
            device_id_type=MESH,
        )

    def swap_wait(part, g):
        own_kv_copy(part, g).wait()
        for d in range(1, slices):
            swap_copy(part, g, d).wait_recv()

    def hops(way, g):
        return half if way == g % 2 else half - 1

    def poll(part, g, s):
        if s == half - 2 and g + 1 < kv_heads:
            swap_wait(part, g + 1)
        for way in range(2):
            if s > hops(way, g):
                continue
            ring_copy(part, way, g, s - 1).wait_recv()
            if s < hops(way, g):
                ring_copy(part, way, g, s).start()
            if s == hops(way, g) - 1 and g + 1 < kv_heads:
                ring_copy(part, way, g + 1, 0).start()

    for g in range(kv_heads):
        for part in range(2):
            for d in range(1, slices):
                swap_copy(part, g, d).start()
    for part in range(2):
        swap_wait(part, 0)
        for way in range(2):
            ring_copy(part, way, 0, 0).start()
    for d in range(1, slices):
        q_copy(0, d).start()

    ends, so_far = [], 0
    for d in range(docs):
        so_far = so_far + docs_ref[d] * BLOCK
        ends.append(so_far)
    starts = []
    for b in range(slices):
        position = b * slot + me * share
        start = jnp.int32(0)
        for end in ends:
            start = jnp.where(end <= position, end, start)
        starts.append(start)

    every = range(slices)
    early, late = [b for b in every if b % 4 in (0, 3)], [b for b in every if b % 4 in (1, 2)]
    steps = [(g, s) for g in range(kv_heads) for s in range(1, half + 1)]
    polls = {t: t + 2 for t in range(len(steps) - 3)}
    for t in range(2):
        for part in range(2):
            poll(part, *steps[t])
    for g in range(1, kv_heads):
        for d in range(1, slices):
            q_copy(g, d).start()
    for t, (g, s) in enumerate(steps):
        if s == 1:
            for d in range(1, slices):
                q_copy(g, d).wait_recv()
            own_q_copy(g).wait()
            update(q_buf, kv_buf, starts, state, g, [me], me, dims, every, True)
        others = [at(-s), at(s)] if s < half else [at(half)]
        if t == len(steps) - 1:
            for part in range(2):
                poll(part, g, s)
        for part, blocks in enumerate((early, late)):
            for b in blocks:
                update(q_buf, kv_buf, starts, state, g, others, me, dims, [b], False)
                if s == half:
                    done = accum[g, b] / jnp.sum(total[g, b], axis=1, keepdims=True)
                    done = done.astype(jnp.bfloat16)
                    for h in range(group):
                        o_buf[g, b, :, h * width:(h + 1) * width] = done[
                            h * share:(h + 1) * share
                        ]
                    pl.when(b != block)(lambda g=g, b=b: o_copy(g, b).start())
            if t in polls:
                poll(part, *steps[polls[t]])
        if s == half:
            out_ref[:, columns((block * kv_heads + g) * wide, wide)] = o_buf[g, block]
    for g in range(kv_heads):
        for d in range(1, slices):
            for part in range(2):
                swap_copy(part, g, d).wait_send()
            q_copy(g, d).wait_send()
        for part in range(2):
            for way in range(2):
                for hop in range(hops(way, g)):
                    ring_copy(part, way, g, hop).wait_send()
        for d in range(1, slices):
            o_copy(g, lax.rem(block + d, slices)).wait()


def by_heads(queries, keys, values, doc_blocks, n_uly, n_blk):
    share = queries.shape[1]
    slot = share * n_uly
    kv_heads = keys.shape[2] // HEAD_WIDTH // n_blk
    group = queries.shape[2] // keys.shape[2]
    docs = doc_blocks.shape[0]
    dims = (n_blk, share, group, slot)
    vmem = pl.BlockSpec(memory_space=pltpu.VMEM)
    anywhere = pl.BlockSpec(memory_space=pl.ANY)
    rows, wide, half = group * share, group * HEAD_WIDTH, n_uly // 2
    dma = pltpu.SemaphoreType.DMA
    out = pl.pallas_call(
        functools.partial(attend, dims, n_uly, kv_heads, docs),
        out_shape=jax.ShapeDtypeStruct(queries.shape[1:], jnp.bfloat16),
        in_specs=[anywhere, anywhere, anywhere, pl.BlockSpec(memory_space=pltpu.SMEM)],
        out_specs=vmem,
        scratch_shapes=[
            pltpu.VMEM((kv_heads, n_blk, share, wide), jnp.bfloat16),
            pltpu.VMEM((2, kv_heads, n_uly, n_blk * share, HEAD_WIDTH), jnp.bfloat16),
            pltpu.VMEM((kv_heads, n_blk, share, wide), jnp.bfloat16),
            pltpu.VMEM((kv_heads, n_blk, rows, HEAD_WIDTH), jnp.float32),
            pltpu.VMEM((kv_heads, n_blk, rows, HEAD_WIDTH), jnp.float32),
            pltpu.VMEM((kv_heads, n_blk, rows, HEAD_WIDTH), jnp.float32),
            dma((2, kv_heads, n_blk - 1)),
            dma((2, kv_heads, n_blk - 1)),
            dma((kv_heads, n_blk - 1)),
            dma((kv_heads, n_blk - 1)),
            dma((2, 2, kv_heads, half)),
            dma((2, 2, kv_heads, half)),
            dma((kv_heads, n_blk - 1)),
            dma((kv_heads, n_blk - 1)),
            dma((2, kv_heads)),
            dma((kv_heads,)),
        ],
        compiler_params=pltpu.CompilerParams(
            collective_id=0, has_side_effects=True, vmem_limit_bytes=60 * 1024 * 1024
        ),
    )(queries[0], keys[0], values[0], doc_blocks)
    return out[None]


def solution(mesh):
    n_uly, n_blk = mesh.shape["uly"], mesh.shape["blk"]

    def on_device(queries, keys, values, doc_blocks):
        if (keys.shape[2] // HEAD_WIDTH) % n_blk == 0 and n_uly % 2 == 0 and n_uly > 4:
            return by_heads(queries, keys, values, doc_blocks, n_uly, n_blk)
        return general(queries, keys, values, doc_blocks)

    return jax.shard_map(
        on_device,
        mesh=mesh,
        in_specs=(
            P(("parts", "blk"), "uly", None),
            P(("parts", "blk"), "uly", None),
            P(("parts", "blk"), "uly", None),
            P("parts"),
        ),
        out_specs=P(("parts", "blk"), "uly", None),
        check_vma=False,
    )
```

```python
import functools
import math

import jax
import jax.numpy as jnp
from jax import lax
from jax.experimental import pallas as pl
from jax.experimental.pallas import tpu as pltpu
from jax.sharding import PartitionSpec as P

HEAD_WIDTH = 128
BLOCK = 128
FAR = 1e30
RATE = math.log2(math.e) / math.sqrt(HEAD_WIDTH)


def segment_of(positions, ends):
    return jnp.sum((positions[:, None] >= ends[None, :]).astype(jnp.int32), axis=1)


def general(queries, keys, values, doc_blocks):
    moved_q, moved_k, moved_v = (
        lax.all_to_all(queries, "uly", split_axis=2, concat_axis=1, tiled=True),
        lax.all_to_all(keys, "uly", split_axis=2, concat_axis=1, tiled=True),
        lax.all_to_all(values, "uly", split_axis=2, concat_axis=1, tiled=True),
    )
    slot = moved_q.shape[1]
    local_q = moved_q.shape[2] // HEAD_WIDTH
    local_kv = moved_k.shape[2] // HEAD_WIDTH
    query_group = local_q // local_kv
    scale = HEAD_WIDTH ** (-0.5)
    first_index = lax.axis_index("blk") * slot
    ends = jnp.cumsum(doc_blocks) * BLOCK
    qpos = first_index + jnp.arange(slot, dtype=jnp.int32)
    qseg = segment_of(qpos, ends)
    qheads = jnp.transpose(moved_q[0].reshape(slot, local_q, HEAD_WIDTH), (1, 0, 2))
    stacked = jnp.concatenate([moved_k, moved_v], axis=0)

    def allowed_for(kpos):
        kseg = segment_of(kpos, ends)
        return (qseg[:, None] == kseg[None, :]) & (kpos[None, :] <= qpos[:, None])

    start_state = (
        jnp.full((local_q, slot), -1e30, jnp.float32),
        jnp.zeros((local_q, slot), jnp.float32),
        jnp.zeros((local_q, slot, HEAD_WIDTH), jnp.float32),
    )
    piece = lax.all_gather(stacked, "blk", axis=1, tiled=True)
    start = jnp.int32(0)
    count = piece.shape[1]

    def work(state):
        key_piece = piece[0].reshape(count, local_kv, HEAD_WIDTH)
        value_piece = piece[1].reshape(count, local_kv, HEAD_WIDTH)
        allowed = allowed_for(jnp.arange(count, dtype=jnp.int32))

        def one_head(inputs):
            head, running, summed, accum = inputs
            qh = lax.dynamic_index_in_dim(qheads, head, 0, keepdims=False)
            kh = lax.dynamic_index_in_dim(key_piece, head // query_group, 1, keepdims=False)
            vh = lax.dynamic_index_in_dim(value_piece, head // query_group, 1, keepdims=False)
            scores = jnp.dot(qh, kh.T, preferred_element_type=jnp.float32) * scale
            scores = jnp.where(allowed, scores, -1e30)
            newest = jnp.maximum(running, jnp.max(scores, axis=1))
            expo = jnp.where(allowed, jnp.exp(scores - newest[:, None]), 0.0)
            factor = jnp.exp(running - newest)
            summed = summed * factor + jnp.sum(expo, axis=1)
            accum = accum * factor[:, None] + jnp.dot(
                expo.astype(jnp.bfloat16), vh, preferred_element_type=jnp.float32
            )
            return (newest, summed, accum)

        return lax.map(one_head, (jnp.arange(local_q, dtype=jnp.int32),) + tuple(state))

    last_seg = jnp.sum((start + count - 1 >= ends).astype(jnp.int32))
    useful = (start < first_index + slot) & (last_seg >= qseg[0])
    running, summed, accum = lax.cond(useful, work, lambda state: state, start_state)
    heads = (accum / summed[:, :, None]).astype(jnp.bfloat16)
    outputs = jnp.transpose(heads, (1, 0, 2)).reshape(1, slot, local_q * HEAD_WIDTH)
    return lax.all_to_all(outputs, "uly", split_axis=1, concat_axis=2, tiled=True)


MESH = pl.DeviceIdType.MESH


def ring_place(device, columns):
    row, side = device // 2, device % 2
    return side * (2 * columns - 1 - row) + (1 - side) * row


def ring_device(place, columns):
    back = place // columns
    return back * ((2 * columns - 1 - place) * 2 + 1) + (1 - back) * (place * 2)


def update(q_buf, kv_buf, starts, state, g, others, me, dims, blocks, first, after=None):
    slices, share, group, slot = dims
    most, total, accum = state
    width = HEAD_WIDTH

    def count_of(b):
        count = (b + 1) * share
        while count * len(others) % width:
            count += share
        return count

    longest = max(count_of(b) for b in blocks)
    bars = []
    for other in others:
        index = lax.broadcasted_iota(jnp.int32, (longest, width), 0)
        column = lax.broadcasted_iota(jnp.int32, (longest, width), 1)
        key = (index // share) * slot + index % share + other * share
        low = jnp.zeros((longest, width), jnp.int32)
        for b in blocks:
            low = jnp.where(column == b, starts[b], low)
        token = column * slot + me * share
        if first:
            token = token + share
        barred = jnp.logical_or(key < low, key >= token)
        barred = jnp.logical_and(barred, column < slices)
        bars.append(jnp.where(barred, jnp.float32(-FAR), jnp.float32(0)).astype(jnp.bfloat16))

    def scores_of(b):
        q = jnp.concatenate(
            [q_buf[g, b, :, h * width:(h + 1) * width] for h in range(group)], axis=0
        )
        pick = lax.broadcasted_iota(jnp.int32, q.shape, 1) == b
        pick = jnp.where(pick, jnp.float32(1), jnp.float32(0)).astype(jnp.bfloat16)
        count = count_of(b)
        k = jnp.concatenate([kv_buf[0, g, other, 0:count, :] for other in others], axis=0)
        bar = jnp.concatenate([bar[:count] for bar in bars], axis=0)
        scores = lax.dot_general(
            jnp.concatenate([q, pick], axis=1), jnp.concatenate([k, bar], axis=1),
            (((1,), (1,)), ((), ())), preferred_element_type=jnp.float32,
        )
        if first:
            row = lax.broadcasted_iota(jnp.int32, scores.shape, 0) % share
            lane = lax.broadcasted_iota(jnp.int32, scores.shape, 1)
            scores = jnp.where(lane <= b * share + row, scores, -FAR)
        return scores

    following = scores_of(blocks[0])
    for i, b in enumerate(blocks):
        scores = following
        if i + 1 < len(blocks):
            following = scores_of(blocks[i + 1])
        count = count_of(b)
        v = jnp.concatenate([kv_buf[1, g, other, 0:count, :] for other in others], axis=0)
        tiles = [scores[:, i:i + width] for i in range(0, scores.shape[1], width)]
        top = jnp.max(functools.reduce(jnp.maximum, tiles), axis=1, keepdims=True)
        top = jnp.broadcast_to(top, (scores.shape[0], width))
        if not first:
            old = most[g, b]
            top = jnp.maximum(top, old)
        weights = [jnp.exp2((tile - top) * RATE) for tile in tiles]
        summed = functools.reduce(jnp.add, weights)
        weights = jnp.concatenate([weight.astype(jnp.bfloat16) for weight in weights], axis=1)
        product = jnp.dot(weights, v, preferred_element_type=jnp.float32)
        if not first:
            factor = jnp.exp2((old - top) * RATE)
            summed = total[g, b] * factor + summed
            product = accum[g, b] * factor + product
        if after is not None:
            after(b, summed, product)
        else:
            most[g, b] = top
            total[g, b] = summed
            accum[g, b] = product


def attend(
    dims, n_uly, kv_heads, docs, q_ref, k_ref, v_ref, docs_ref, out_ref,
    q_buf, kv_buf, o_buf, most, total, accum,
    swap_send, swap_recv, q_send, q_recv, ring_send, ring_recv, o_send, o_recv, own_kv, own_q,
):
    slices, share, group, slot = dims
    width = HEAD_WIDTH
    half = n_uly // 2
    me, block = lax.axis_index("uly"), lax.axis_index("blk")
    place = ring_place(me, half)
    at = lambda offset: ring_device(lax.rem(place + offset + n_uly, n_uly), half)
    ahead, behind = at(1), at(-1)
    state = (most, total, accum)
    wide = group * width

    def rows(b):
        return pl.ds(pl.multiple_of(b * share, share), share)

    def columns(start, size):
        return pl.ds(pl.multiple_of(start, width), size)

    def own_kv_copy(part, g):
        return pltpu.make_async_copy(
            (k_ref, v_ref)[part].at[:, columns((block * kv_heads + g) * width, width)],
            kv_buf.at[part, g, me, rows(block), :],
            own_kv.at[part, g],
        )

    def own_q_copy(g):
        return pltpu.make_async_copy(
            q_ref.at[:, columns((block * kv_heads + g) * wide, wide)],
            q_buf.at[g, block],
            own_q.at[g],
        )

    for g in range(kv_heads):
        for part in range(2):
            own_kv_copy(part, g).start()
        own_q_copy(g).start()

    barrier = pltpu.get_barrier_semaphore()
    for other in (ahead, behind):
        pl.semaphore_signal(barrier, inc=1, device_id={"uly": other}, device_id_type=MESH)
    for d in range(1, slices):
        peer = lax.rem(block + d, slices)
        pl.semaphore_signal(barrier, inc=1, device_id={"blk": peer}, device_id_type=MESH)
    pl.semaphore_wait(barrier, slices + 1)

    def swap_copy(part, g, d):
        peer = lax.rem(block + d, slices)
        return pltpu.make_async_remote_copy(
            src_ref=(k_ref, v_ref)[part].at[:, columns((peer * kv_heads + g) * width, width)],
            dst_ref=kv_buf.at[part, g, me, rows(block), :],
            send_sem=swap_send.at[part, g, d - 1],
            recv_sem=swap_recv.at[part, g, d - 1],
            device_id={"blk": peer},
            device_id_type=MESH,
        )

    def q_copy(g, d):
        peer = lax.rem(block + d, slices)
        return pltpu.make_async_remote_copy(
            src_ref=q_ref.at[:, columns((peer * kv_heads + g) * wide, wide)],
            dst_ref=q_buf.at[g, block],
            send_sem=q_send.at[g, d - 1],
            recv_sem=q_recv.at[g, d - 1],
            device_id={"blk": peer},
            device_id_type=MESH,
        )

    def o_copy(g, peer):
        d = lax.rem(peer - block + slices, slices)
        return pltpu.make_async_remote_copy(
            src_ref=o_buf.at[g, peer],
            dst_ref=out_ref.at[:, columns((block * kv_heads + g) * wide, wide)],
            send_sem=o_send.at[g, d - 1],
            recv_sem=o_recv.at[g, d - 1],
            device_id={"blk": peer},
            device_id_type=MESH,
        )

    def ring_copy(part, way, g, hop):
        origin = at(-hop) if way == 0 else at(hop)
        tile = kv_buf.at[part, g, origin]
        return pltpu.make_async_remote_copy(
            src_ref=tile,
            dst_ref=tile,
            send_sem=ring_send.at[part, way, g, hop],
            recv_sem=ring_recv.at[part, way, g, hop],
            device_id={"uly": ahead if way == 0 else behind},
            device_id_type=MESH,
        )

    def swap_wait(part, g):
        own_kv_copy(part, g).wait()
        for d in range(1, slices):
            swap_copy(part, g, d).wait_recv()

    def hops(way, g):
        return half if way == g % 2 else half - 1

    def poll(part, g, s):
        if s == half - 2 and g + 1 < kv_heads:
            swap_wait(part, g + 1)
        for way in range(2):
            if s > hops(way, g):
                continue
            ring_copy(part, way, g, s - 1).wait_recv()
            if s < hops(way, g):
                ring_copy(part, way, g, s).start()
            if s == hops(way, g) - 1 and g + 1 < kv_heads:
                ring_copy(part, way, g + 1, 0).start()

    for g in range(kv_heads):
        for part in range(2):
            for d in range(1, slices):
                swap_copy(part, g, d).start()
    for part in range(2):
        swap_wait(part, 0)
        for way in range(2):
            ring_copy(part, way, 0, 0).start()
    for d in range(1, slices):
        q_copy(0, d).start()

    ends, so_far = [], 0
    for d in range(docs):
        so_far = so_far + docs_ref[d] * BLOCK
        ends.append(so_far)
    starts = []
    for b in range(slices):
        position = b * slot + me * share
        start = jnp.int32(0)
        for end in ends:
            start = jnp.where(end <= position, end, start)
        starts.append(start)

    every = list(range(slices))[::-1]
    early, late = [b for b in every if b % 4 in (0, 3)], [b for b in every if b % 4 in (1, 2)]
    steps = [(g, s) for g in range(kv_heads) for s in range(1, half + 1)]
    polls = {t: t + 2 for t in range(len(steps) - 3)}
    for t in range(2):
        for part in range(2):
            poll(part, *steps[t])
    for g in range(1, kv_heads):
        for d in range(1, slices):
            q_copy(g, d).start()
    for t, (g, s) in enumerate(steps):
        if s == 1:
            for d in range(1, slices):
                q_copy(g, d).wait_recv()
            own_q_copy(g).wait()
            update(q_buf, kv_buf, starts, state, g, [me], me, dims, every, True)
        others = [at(-s), at(s)] if s < half else [at(half)]
        if t == len(steps) - 1:
            for part in range(2):
                poll(part, g, s)

        def leave(b, summed, product, g=g):
            done = product / jnp.sum(summed, axis=1, keepdims=True)
            done = done.astype(jnp.bfloat16)
            for h in range(group):
                o_buf[g, b, :, h * width:(h + 1) * width] = done[h * share:(h + 1) * share]

        if s < half:
            update(q_buf, kv_buf, starts, state, g, others, me, dims, every, False)
        else:
            for pair in (early, late):
                update(q_buf, kv_buf, starts, state, g, others, me, dims, pair, False, leave)
                for b in pair:
                    pl.when(b != block)(lambda g=g, b=b: o_copy(g, b).start())
        if t in polls:
            for part in range(2):
                poll(part, *steps[polls[t]])
        if s == half:
            out_ref[:, columns((block * kv_heads + g) * wide, wide)] = o_buf[g, block]
    for g in range(kv_heads):
        for d in range(1, slices):
            for part in range(2):
                swap_copy(part, g, d).wait_send()
            q_copy(g, d).wait_send()
        for part in range(2):
            for way in range(2):
                for hop in range(hops(way, g)):
                    ring_copy(part, way, g, hop).wait_send()
        for d in range(1, slices):
            o_copy(g, lax.rem(block + d, slices)).wait()


def hand_over(from_ref, to_ref, done):
    size = from_ref.shape[0] // 4
    pieces = [pl.ds(i * size, size) for i in range(4)]
    copies = [
        pltpu.make_async_copy(from_ref.at[piece], to_ref.at[piece], done.at[i])
        for i, piece in enumerate(pieces)
    ]
    for copy in copies:
        copy.start()
    for copy in copies:
        copy.wait()


def by_heads(queries, keys, values, doc_blocks, n_uly, n_blk):
    share = queries.shape[1]
    slot = share * n_uly
    kv_heads = keys.shape[2] // HEAD_WIDTH // n_blk
    group = queries.shape[2] // keys.shape[2]
    docs = doc_blocks.shape[0]
    dims = (n_blk, share, group, slot)
    vmem = pl.BlockSpec(memory_space=pltpu.VMEM)
    anywhere = pl.BlockSpec(memory_space=pl.ANY)
    rows, wide, half = group * share, group * HEAD_WIDTH, n_uly // 2
    dma = pltpu.SemaphoreType.DMA
    out = pl.pallas_call(
        functools.partial(attend, dims, n_uly, kv_heads, docs),
        out_shape=jax.ShapeDtypeStruct(queries.shape[1:], jnp.bfloat16),
        in_specs=[anywhere, anywhere, anywhere, pl.BlockSpec(memory_space=pltpu.SMEM)],
        out_specs=vmem,
        scratch_shapes=[
            pltpu.VMEM((kv_heads, n_blk, share, wide), jnp.bfloat16),
            pltpu.VMEM((2, kv_heads, n_uly, n_blk * share, HEAD_WIDTH), jnp.bfloat16),
            pltpu.VMEM((kv_heads, n_blk, share, wide), jnp.bfloat16),
            pltpu.VMEM((kv_heads, n_blk, rows, HEAD_WIDTH), jnp.float32),
            pltpu.VMEM((kv_heads, n_blk, rows, HEAD_WIDTH), jnp.float32),
            pltpu.VMEM((kv_heads, n_blk, rows, HEAD_WIDTH), jnp.float32),
            dma((2, kv_heads, n_blk - 1)),
            dma((2, kv_heads, n_blk - 1)),
            dma((kv_heads, n_blk - 1)),
            dma((kv_heads, n_blk - 1)),
            dma((2, 2, kv_heads, half)),
            dma((2, 2, kv_heads, half)),
            dma((kv_heads, n_blk - 1)),
            dma((kv_heads, n_blk - 1)),
            dma((2, kv_heads)),
            dma((kv_heads,)),
        ],
        compiler_params=pltpu.CompilerParams(
            collective_id=0, has_side_effects=True, vmem_limit_bytes=60 * 1024 * 1024
        ),
    )(queries[0], keys[0], values[0], doc_blocks)
    return pl.pallas_call(
        hand_over,
        out_shape=jax.ShapeDtypeStruct(out.shape, out.dtype),
        in_specs=[anywhere],
        out_specs=anywhere,
        scratch_shapes=[dma((4,))],
        compiler_params=pltpu.CompilerParams(vmem_limit_bytes=60 * 1024 * 1024),
    )(out)[None]


def solution(mesh):
    n_uly, n_blk = mesh.shape["uly"], mesh.shape["blk"]

    def on_device(queries, keys, values, doc_blocks):
        if (keys.shape[2] // HEAD_WIDTH) % n_blk == 0 and n_uly % 2 == 0 and n_uly > 4:
            return by_heads(queries, keys, values, doc_blocks, n_uly, n_blk)
        return general(queries, keys, values, doc_blocks)

    return jax.shard_map(
        on_device,
        mesh=mesh,
        in_specs=(
            P(("parts", "blk"), "uly", None),
            P(("parts", "blk"), "uly", None),
            P(("parts", "blk"), "uly", None),
            P("parts"),
        ),
        out_specs=P(("parts", "blk"), "uly", None),
        check_vma=False,
    )
```

```python
import functools
import math

import jax
import jax.numpy as jnp
from jax import lax
from jax.experimental import pallas as pl
from jax.experimental.pallas import tpu as pltpu
from jax.sharding import PartitionSpec as P

HEAD_WIDTH = 128
BLOCK = 128
FAR = 1e30
RATE = math.log2(math.e) / math.sqrt(HEAD_WIDTH)


def segment_of(positions, ends):
    return jnp.sum((positions[:, None] >= ends[None, :]).astype(jnp.int32), axis=1)


def general(queries, keys, values, doc_blocks):
    moved_q, moved_k, moved_v = (
        lax.all_to_all(queries, "uly", split_axis=2, concat_axis=1, tiled=True),
        lax.all_to_all(keys, "uly", split_axis=2, concat_axis=1, tiled=True),
        lax.all_to_all(values, "uly", split_axis=2, concat_axis=1, tiled=True),
    )
    slot = moved_q.shape[1]
    local_q = moved_q.shape[2] // HEAD_WIDTH
    local_kv = moved_k.shape[2] // HEAD_WIDTH
    query_group = local_q // local_kv
    scale = HEAD_WIDTH ** (-0.5)
    first_index = lax.axis_index("blk") * slot
    ends = jnp.cumsum(doc_blocks) * BLOCK
    qpos = first_index + jnp.arange(slot, dtype=jnp.int32)
    qseg = segment_of(qpos, ends)
    qheads = jnp.transpose(moved_q[0].reshape(slot, local_q, HEAD_WIDTH), (1, 0, 2))
    stacked = jnp.concatenate([moved_k, moved_v], axis=0)

    def allowed_for(kpos):
        kseg = segment_of(kpos, ends)
        return (qseg[:, None] == kseg[None, :]) & (kpos[None, :] <= qpos[:, None])

    start_state = (
        jnp.full((local_q, slot), -1e30, jnp.float32),
        jnp.zeros((local_q, slot), jnp.float32),
        jnp.zeros((local_q, slot, HEAD_WIDTH), jnp.float32),
    )
    piece = lax.all_gather(stacked, "blk", axis=1, tiled=True)
    start = jnp.int32(0)
    count = piece.shape[1]

    def work(state):
        key_piece = piece[0].reshape(count, local_kv, HEAD_WIDTH)
        value_piece = piece[1].reshape(count, local_kv, HEAD_WIDTH)
        allowed = allowed_for(jnp.arange(count, dtype=jnp.int32))

        def one_head(inputs):
            head, running, summed, accum = inputs
            qh = lax.dynamic_index_in_dim(qheads, head, 0, keepdims=False)
            kh = lax.dynamic_index_in_dim(key_piece, head // query_group, 1, keepdims=False)
            vh = lax.dynamic_index_in_dim(value_piece, head // query_group, 1, keepdims=False)
            scores = jnp.dot(qh, kh.T, preferred_element_type=jnp.float32) * scale
            scores = jnp.where(allowed, scores, -1e30)
            newest = jnp.maximum(running, jnp.max(scores, axis=1))
            expo = jnp.where(allowed, jnp.exp(scores - newest[:, None]), 0.0)
            factor = jnp.exp(running - newest)
            summed = summed * factor + jnp.sum(expo, axis=1)
            accum = accum * factor[:, None] + jnp.dot(
                expo.astype(jnp.bfloat16), vh, preferred_element_type=jnp.float32
            )
            return (newest, summed, accum)

        return lax.map(one_head, (jnp.arange(local_q, dtype=jnp.int32),) + tuple(state))

    last_seg = jnp.sum((start + count - 1 >= ends).astype(jnp.int32))
    useful = (start < first_index + slot) & (last_seg >= qseg[0])
    running, summed, accum = lax.cond(useful, work, lambda state: state, start_state)
    heads = (accum / summed[:, :, None]).astype(jnp.bfloat16)
    outputs = jnp.transpose(heads, (1, 0, 2)).reshape(1, slot, local_q * HEAD_WIDTH)
    return lax.all_to_all(outputs, "uly", split_axis=1, concat_axis=2, tiled=True)


MESH = pl.DeviceIdType.MESH


def ring_place(device, columns):
    row, side = device // 2, device % 2
    return side * (2 * columns - 1 - row) + (1 - side) * row


def ring_device(place, columns):
    back = place // columns
    return back * ((2 * columns - 1 - place) * 2 + 1) + (1 - back) * (place * 2)


def update(q_buf, kv_buf, starts, state, g, others, me, dims, blocks, first):
    slices, share, group, slot = dims
    most, total, accum = state
    for b in blocks:
        q = jnp.concatenate(
            [q_buf[g, b, :, h * HEAD_WIDTH:(h + 1) * HEAD_WIDTH] for h in range(group)], axis=0
        )
        count = (b + 1) * share
        while count * len(others) % HEAD_WIDTH:
            count += share
        k = jnp.concatenate([kv_buf[0, g, other, 0:count, :] for other in others], axis=0)
        v = jnp.concatenate([kv_buf[1, g, other, 0:count, :] for other in others], axis=0)
        scores = lax.dot_general(
            q, k, (((1,), (1,)), ((), ())), preferred_element_type=jnp.float32
        )
        size = k.shape[0]
        token = b * slot + me * share
        lane = lax.broadcasted_iota(jnp.int32, (1, size), 1)
        index = lane % count
        origin = jnp.where(lane < count, others[0], others[-1])
        key = (index // share) * slot + index % share + origin * share
        allowed = key >= starts[b]
        if first:
            row = lax.broadcasted_iota(jnp.int32, scores.shape, 0) % share
            scores = jnp.where(jnp.logical_and(allowed, key <= token + row), scores, -FAR)
        else:
            allowed = jnp.logical_and(allowed, key < token)
            scores = scores + jnp.where(allowed, jnp.float32(0), jnp.float32(-FAR))
        tiles = [scores[:, i:i + HEAD_WIDTH] for i in range(0, size, HEAD_WIDTH)]
        top = jnp.max(functools.reduce(jnp.maximum, tiles), axis=1, keepdims=True)
        top = jnp.broadcast_to(top, (scores.shape[0], HEAD_WIDTH))
        if not first:
            old = most[g, b]
            top = jnp.maximum(top, old)
        weights = [jnp.exp2((tile - top) * RATE) for tile in tiles]
        summed = functools.reduce(jnp.add, weights)
        weights = jnp.concatenate([weight.astype(jnp.bfloat16) for weight in weights], axis=1)
        product = jnp.dot(weights, v, preferred_element_type=jnp.float32)
        most[g, b] = top
        if first:
            total[g, b] = summed
            accum[g, b] = product
        else:
            factor = jnp.exp2((old - top) * RATE)
            total[g, b] = total[g, b] * factor + summed
            accum[g, b] = accum[g, b] * factor + product


def attend(
    dims, n_uly, kv_heads, docs, q_ref, k_ref, v_ref, docs_ref, out_ref,
    q_buf, kv_buf, o_buf, most, total, accum,
    swap_send, swap_recv, q_send, q_recv, ring_send, ring_recv, o_send, o_recv, own_kv, own_q,
):
    slices, share, group, slot = dims
    width = HEAD_WIDTH
    half = n_uly // 2
    me, block = lax.axis_index("uly"), lax.axis_index("blk")
    place = ring_place(me, half)
    at = lambda offset: ring_device(lax.rem(place + offset + n_uly, n_uly), half)
    ahead, behind = at(1), at(-1)
    state = (most, total, accum)
    wide = group * width

    def rows(b):
        return pl.ds(pl.multiple_of(b * share, share), share)

    def columns(start, size):
        return pl.ds(pl.multiple_of(start, width), size)

    def own_kv_copy(part, g):
        return pltpu.make_async_copy(
            (k_ref, v_ref)[part].at[:, columns((block * kv_heads + g) * width, width)],
            kv_buf.at[part, g, me, rows(block), :],
            own_kv.at[part, g],
        )

    def own_q_copy(g):
        return pltpu.make_async_copy(
            q_ref.at[:, columns((block * kv_heads + g) * wide, wide)],
            q_buf.at[g, block],
            own_q.at[g],
        )

    for g in range(kv_heads):
        for part in range(2):
            own_kv_copy(part, g).start()
        own_q_copy(g).start()

    barrier = pltpu.get_barrier_semaphore()
    for other in (ahead, behind):
        pl.semaphore_signal(barrier, inc=1, device_id={"uly": other}, device_id_type=MESH)
    for d in range(1, slices):
        peer = lax.rem(block + d, slices)
        pl.semaphore_signal(barrier, inc=1, device_id={"blk": peer}, device_id_type=MESH)
    pl.semaphore_wait(barrier, slices + 1)

    def swap_copy(part, g, d):
        peer = lax.rem(block + d, slices)
        return pltpu.make_async_remote_copy(
            src_ref=(k_ref, v_ref)[part].at[:, columns((peer * kv_heads + g) * width, width)],
            dst_ref=kv_buf.at[part, g, me, rows(block), :],
            send_sem=swap_send.at[part, g, d - 1],
            recv_sem=swap_recv.at[part, g, d - 1],
            device_id={"blk": peer},
            device_id_type=MESH,
        )

    def q_copy(g, d):
        peer = lax.rem(block + d, slices)
        return pltpu.make_async_remote_copy(
            src_ref=q_ref.at[:, columns((peer * kv_heads + g) * wide, wide)],
            dst_ref=q_buf.at[g, block],
            send_sem=q_send.at[g, d - 1],
            recv_sem=q_recv.at[g, d - 1],
            device_id={"blk": peer},
            device_id_type=MESH,
        )

    def o_copy(g, peer):
        d = lax.rem(peer - block + slices, slices)
        return pltpu.make_async_remote_copy(
            src_ref=o_buf.at[g, peer],
            dst_ref=out_ref.at[:, columns((block * kv_heads + g) * wide, wide)],
            send_sem=o_send.at[g, d - 1],
            recv_sem=o_recv.at[g, d - 1],
            device_id={"blk": peer},
            device_id_type=MESH,
        )

    def ring_copy(part, way, g, hop):
        origin = at(-hop) if way == 0 else at(hop)
        tile = kv_buf.at[part, g, origin]
        return pltpu.make_async_remote_copy(
            src_ref=tile,
            dst_ref=tile,
            send_sem=ring_send.at[part, way, g, hop],
            recv_sem=ring_recv.at[part, way, g, hop],
            device_id={"uly": ahead if way == 0 else behind},
            device_id_type=MESH,
        )

    def swap_wait(part, g):
        own_kv_copy(part, g).wait()
        for d in range(1, slices):
            swap_copy(part, g, d).wait_recv()

    def hops(way, g):
        return half if way == g % 2 else half - 1

    def poll(part, g, s):
        if s == half - 2 and g + 1 < kv_heads:
            swap_wait(part, g + 1)
        for way in range(2):
            if s > hops(way, g):
                continue
            ring_copy(part, way, g, s - 1).wait_recv()
            if s < hops(way, g):
                ring_copy(part, way, g, s).start()
            if s == hops(way, g) - 1 and g + 1 < kv_heads:
                ring_copy(part, way, g + 1, 0).start()

    for g in range(kv_heads):
        for part in range(2):
            for d in range(1, slices):
                swap_copy(part, g, d).start()
    for part in range(2):
        swap_wait(part, 0)
        for way in range(2):
            ring_copy(part, way, 0, 0).start()
    for d in range(1, slices):
        q_copy(0, d).start()

    ends, so_far = [], 0
    for d in range(docs):
        so_far = so_far + docs_ref[d] * BLOCK
        ends.append(so_far)
    starts = []
    for b in range(slices):
        position = b * slot + me * share
        start = jnp.int32(0)
        for end in ends:
            start = jnp.where(end <= position, end, start)
        starts.append(start)

    every = range(slices)
    early, late = [b for b in every if b % 4 in (0, 3)], [b for b in every if b % 4 in (1, 2)]
    steps = [(g, s) for g in range(kv_heads) for s in range(1, half + 1)]
    polls = {t: t + 2 for t in range(len(steps) - 3)}
    for t in range(2):
        for part in range(2):
            poll(part, *steps[t])
    for g in range(1, kv_heads):
        for d in range(1, slices):
            q_copy(g, d).start()
    for t, (g, s) in enumerate(steps):
        if s == 1:
            for d in range(1, slices):
                q_copy(g, d).wait_recv()
            own_q_copy(g).wait()
            update(q_buf, kv_buf, starts, state, g, [me], me, dims, every, True)
        others = [at(-s), at(s)] if s < half else [at(half)]
        if t == len(steps) - 1:
            for part in range(2):
                poll(part, g, s)
        for part, blocks in enumerate((early, late)):
            for b in blocks:
                update(q_buf, kv_buf, starts, state, g, others, me, dims, [b], False)
                if s == half:
                    done = accum[g, b] / jnp.sum(total[g, b], axis=1, keepdims=True)
                    done = done.astype(jnp.bfloat16)
                    for h in range(group):
                        o_buf[g, b, :, h * width:(h + 1) * width] = done[
                            h * share:(h + 1) * share
                        ]
                    pl.when(b != block)(lambda g=g, b=b: o_copy(g, b).start())
            if t in polls:
                poll(part, *steps[polls[t]])
        if s == half:
            out_ref[:, columns((block * kv_heads + g) * wide, wide)] = o_buf[g, block]
    for g in range(kv_heads):
        for d in range(1, slices):
            for part in range(2):
                swap_copy(part, g, d).wait_send()
            q_copy(g, d).wait_send()
        for part in range(2):
            for way in range(2):
                for hop in range(hops(way, g)):
                    ring_copy(part, way, g, hop).wait_send()
        for d in range(1, slices):
            o_copy(g, lax.rem(block + d, slices)).wait()


def hand_over(from_ref, to_ref):
    to_ref[...] = from_ref[...]


def by_heads(queries, keys, values, doc_blocks, n_uly, n_blk):
    share = queries.shape[1]
    slot = share * n_uly
    kv_heads = keys.shape[2] // HEAD_WIDTH // n_blk
    group = queries.shape[2] // keys.shape[2]
    docs = doc_blocks.shape[0]
    dims = (n_blk, share, group, slot)
    vmem = pl.BlockSpec(memory_space=pltpu.VMEM)
    anywhere = pl.BlockSpec(memory_space=pl.ANY)
    rows, wide, half = group * share, group * HEAD_WIDTH, n_uly // 2
    dma = pltpu.SemaphoreType.DMA
    out = pl.pallas_call(
        functools.partial(attend, dims, n_uly, kv_heads, docs),
        out_shape=jax.ShapeDtypeStruct(queries.shape[1:], jnp.bfloat16),
        in_specs=[anywhere, anywhere, anywhere, pl.BlockSpec(memory_space=pltpu.SMEM)],
        out_specs=vmem,
        scratch_shapes=[
            pltpu.VMEM((kv_heads, n_blk, share, wide), jnp.bfloat16),
            pltpu.VMEM((2, kv_heads, n_uly, n_blk * share, HEAD_WIDTH), jnp.bfloat16),
            pltpu.VMEM((kv_heads, n_blk, share, wide), jnp.bfloat16),
            pltpu.VMEM((kv_heads, n_blk, rows, HEAD_WIDTH), jnp.float32),
            pltpu.VMEM((kv_heads, n_blk, rows, HEAD_WIDTH), jnp.float32),
            pltpu.VMEM((kv_heads, n_blk, rows, HEAD_WIDTH), jnp.float32),
            dma((2, kv_heads, n_blk - 1)),
            dma((2, kv_heads, n_blk - 1)),
            dma((kv_heads, n_blk - 1)),
            dma((kv_heads, n_blk - 1)),
            dma((2, 2, kv_heads, half)),
            dma((2, 2, kv_heads, half)),
            dma((kv_heads, n_blk - 1)),
            dma((kv_heads, n_blk - 1)),
            dma((2, kv_heads)),
            dma((kv_heads,)),
        ],
        compiler_params=pltpu.CompilerParams(
            collective_id=0, has_side_effects=True, vmem_limit_bytes=60 * 1024 * 1024
        ),
    )(queries[0], keys[0], values[0], doc_blocks)
    piece = pl.BlockSpec((out.shape[0] // 4, out.shape[1]), lambda i: (i, 0))
    return pl.pallas_call(
        hand_over,
        grid=(4,),
        out_shape=jax.ShapeDtypeStruct(out.shape, out.dtype),
        in_specs=[piece],
        out_specs=piece,
        compiler_params=pltpu.CompilerParams(vmem_limit_bytes=60 * 1024 * 1024),
    )(out)[None]


def solution(mesh):
    n_uly, n_blk = mesh.shape["uly"], mesh.shape["blk"]

    def on_device(queries, keys, values, doc_blocks):
        if (keys.shape[2] // HEAD_WIDTH) % n_blk == 0 and n_uly % 2 == 0 and n_uly > 4:
            return by_heads(queries, keys, values, doc_blocks, n_uly, n_blk)
        return general(queries, keys, values, doc_blocks)

    return jax.shard_map(
        on_device,
        mesh=mesh,
        in_specs=(
            P(("parts", "blk"), "uly", None),
            P(("parts", "blk"), "uly", None),
            P(("parts", "blk"), "uly", None),
            P("parts"),
        ),
        out_specs=P(("parts", "blk"), "uly", None),
        check_vma=False,
    )
```

```python
import functools
import math

import jax
import jax.numpy as jnp
from jax import lax
from jax.experimental import pallas as pl
from jax.experimental.pallas import tpu as pltpu
from jax.sharding import PartitionSpec as P

HEAD_WIDTH = 128
BLOCK = 128
FAR = 1e30
RATE = math.log2(math.e) / math.sqrt(HEAD_WIDTH)


def segment_of(positions, ends):
    return jnp.sum((positions[:, None] >= ends[None, :]).astype(jnp.int32), axis=1)


def general(queries, keys, values, doc_blocks):
    moved_q, moved_k, moved_v = (
        lax.all_to_all(queries, "uly", split_axis=2, concat_axis=1, tiled=True),
        lax.all_to_all(keys, "uly", split_axis=2, concat_axis=1, tiled=True),
        lax.all_to_all(values, "uly", split_axis=2, concat_axis=1, tiled=True),
    )
    slot = moved_q.shape[1]
    local_q = moved_q.shape[2] // HEAD_WIDTH
    local_kv = moved_k.shape[2] // HEAD_WIDTH
    query_group = local_q // local_kv
    scale = HEAD_WIDTH ** (-0.5)
    first_index = lax.axis_index("blk") * slot
    ends = jnp.cumsum(doc_blocks) * BLOCK
    qpos = first_index + jnp.arange(slot, dtype=jnp.int32)
    qseg = segment_of(qpos, ends)
    qheads = jnp.transpose(moved_q[0].reshape(slot, local_q, HEAD_WIDTH), (1, 0, 2))
    stacked = jnp.concatenate([moved_k, moved_v], axis=0)

    def allowed_for(kpos):
        kseg = segment_of(kpos, ends)
        return (qseg[:, None] == kseg[None, :]) & (kpos[None, :] <= qpos[:, None])

    start_state = (
        jnp.full((local_q, slot), -1e30, jnp.float32),
        jnp.zeros((local_q, slot), jnp.float32),
        jnp.zeros((local_q, slot, HEAD_WIDTH), jnp.float32),
    )
    piece = lax.all_gather(stacked, "blk", axis=1, tiled=True)
    start = jnp.int32(0)
    count = piece.shape[1]

    def work(state):
        key_piece = piece[0].reshape(count, local_kv, HEAD_WIDTH)
        value_piece = piece[1].reshape(count, local_kv, HEAD_WIDTH)
        allowed = allowed_for(jnp.arange(count, dtype=jnp.int32))

        def one_head(inputs):
            head, running, summed, accum = inputs
            qh = lax.dynamic_index_in_dim(qheads, head, 0, keepdims=False)
            kh = lax.dynamic_index_in_dim(key_piece, head // query_group, 1, keepdims=False)
            vh = lax.dynamic_index_in_dim(value_piece, head // query_group, 1, keepdims=False)
            scores = jnp.dot(qh, kh.T, preferred_element_type=jnp.float32) * scale
            scores = jnp.where(allowed, scores, -1e30)
            newest = jnp.maximum(running, jnp.max(scores, axis=1))
            expo = jnp.where(allowed, jnp.exp(scores - newest[:, None]), 0.0)
            factor = jnp.exp(running - newest)
            summed = summed * factor + jnp.sum(expo, axis=1)
            accum = accum * factor[:, None] + jnp.dot(
                expo.astype(jnp.bfloat16), vh, preferred_element_type=jnp.float32
            )
            return (newest, summed, accum)

        return lax.map(one_head, (jnp.arange(local_q, dtype=jnp.int32),) + tuple(state))

    last_seg = jnp.sum((start + count - 1 >= ends).astype(jnp.int32))
    useful = (start < first_index + slot) & (last_seg >= qseg[0])
    running, summed, accum = lax.cond(useful, work, lambda state: state, start_state)
    heads = (accum / summed[:, :, None]).astype(jnp.bfloat16)
    outputs = jnp.transpose(heads, (1, 0, 2)).reshape(1, slot, local_q * HEAD_WIDTH)
    return lax.all_to_all(outputs, "uly", split_axis=1, concat_axis=2, tiled=True)


MESH = pl.DeviceIdType.MESH


def ring_place(device, columns):
    row, side = device // 2, device % 2
    return side * (2 * columns - 1 - row) + (1 - side) * row


def ring_device(place, columns):
    back = place // columns
    return back * ((2 * columns - 1 - place) * 2 + 1) + (1 - back) * (place * 2)


def update(q_buf, kv_buf, starts, state, g, others, me, dims, blocks, first):
    slices, share, group, slot = dims
    most, total, accum = state
    for b in blocks:
        q = jnp.concatenate(
            [q_buf[g, b, :, h * HEAD_WIDTH:(h + 1) * HEAD_WIDTH] for h in range(group)], axis=0
        )
        count = (b + 1) * share
        while count * len(others) % HEAD_WIDTH:
            count += share
        k = jnp.concatenate([kv_buf[0, g, other, 0:count, :] for other in others], axis=0)
        v = jnp.concatenate([kv_buf[1, g, other, 0:count, :] for other in others], axis=0)
        scores = lax.dot_general(
            q, k, (((1,), (1,)), ((), ())), preferred_element_type=jnp.float32
        )
        size = k.shape[0]
        token = b * slot + me * share
        lane = lax.broadcasted_iota(jnp.int32, (1, size), 1)
        index = lane % count
        origin = jnp.where(lane < count, others[0], others[-1])
        key = (index // share) * slot + index % share + origin * share
        allowed = key >= starts[b]
        if first:
            row = lax.broadcasted_iota(jnp.int32, scores.shape, 0) % share
            scores = jnp.where(jnp.logical_and(allowed, key <= token + row), scores, -FAR)
        else:
            allowed = jnp.logical_and(allowed, key < token)
            scores = scores + jnp.where(allowed, jnp.float32(0), jnp.float32(-FAR))
        tiles = [scores[:, i:i + HEAD_WIDTH] for i in range(0, size, HEAD_WIDTH)]
        top = jnp.max(functools.reduce(jnp.maximum, tiles), axis=1, keepdims=True)
        top = jnp.broadcast_to(top, (scores.shape[0], HEAD_WIDTH))
        if not first:
            old = most[g, b]
            top = jnp.maximum(top, old)
        weights = [jnp.exp2((tile - top) * RATE) for tile in tiles]
        summed = functools.reduce(jnp.add, weights)
        weights = jnp.concatenate([weight.astype(jnp.bfloat16) for weight in weights], axis=1)
        product = jnp.dot(weights, v, preferred_element_type=jnp.float32)
        most[g, b] = top
        if first:
            total[g, b] = summed
            accum[g, b] = product
        else:
            factor = jnp.exp2((old - top) * RATE)
            total[g, b] = total[g, b] * factor + summed
            accum[g, b] = accum[g, b] * factor + product


def attend(
    dims, n_uly, kv_heads, docs, q_ref, k_ref, v_ref, docs_ref, out_ref,
    q_buf, kv_buf, o_buf, most, total, accum,
    swap_send, swap_recv, q_send, q_recv, ring_send, ring_recv, o_send, o_recv, own_kv, own_q,
):
    slices, share, group, slot = dims
    width = HEAD_WIDTH
    half = n_uly // 2
    me, block = lax.axis_index("uly"), lax.axis_index("blk")
    place = ring_place(me, half)
    at = lambda offset: ring_device(lax.rem(place + offset + n_uly, n_uly), half)
    ahead, behind = at(1), at(-1)
    state = (most, total, accum)
    wide = group * width

    def rows(b):
        return pl.ds(pl.multiple_of(b * share, share), share)

    def columns(start, size):
        return pl.ds(pl.multiple_of(start, width), size)

    def own_kv_copy(part, g):
        return pltpu.make_async_copy(
            (k_ref, v_ref)[part].at[:, columns((block * kv_heads + g) * width, width)],
            kv_buf.at[part, g, me, rows(block), :],
            own_kv.at[part, g],
        )

    def own_q_copy(g):
        return pltpu.make_async_copy(
            q_ref.at[:, columns((block * kv_heads + g) * wide, wide)],
            q_buf.at[g, block],
            own_q.at[g],
        )

    for g in range(kv_heads):
        for part in range(2):
            own_kv_copy(part, g).start()
        own_q_copy(g).start()

    barrier = pltpu.get_barrier_semaphore()
    for other in (ahead, behind):
        pl.semaphore_signal(barrier, inc=1, device_id={"uly": other}, device_id_type=MESH)
    for d in range(1, slices):
        peer = lax.rem(block + d, slices)
        pl.semaphore_signal(barrier, inc=1, device_id={"blk": peer}, device_id_type=MESH)
    pl.semaphore_wait(barrier, slices + 1)

    def swap_copy(part, g, d):
        peer = lax.rem(block + d, slices)
        return pltpu.make_async_remote_copy(
            src_ref=(k_ref, v_ref)[part].at[:, columns((peer * kv_heads + g) * width, width)],
            dst_ref=kv_buf.at[part, g, me, rows(block), :],
            send_sem=swap_send.at[part, g, d - 1],
            recv_sem=swap_recv.at[part, g, d - 1],
            device_id={"blk": peer},
            device_id_type=MESH,
        )

    def q_copy(g, d):
        peer = lax.rem(block + d, slices)
        return pltpu.make_async_remote_copy(
            src_ref=q_ref.at[:, columns((peer * kv_heads + g) * wide, wide)],
            dst_ref=q_buf.at[g, block],
            send_sem=q_send.at[g, d - 1],
            recv_sem=q_recv.at[g, d - 1],
            device_id={"blk": peer},
            device_id_type=MESH,
        )

    def o_copy(g, peer):
        d = lax.rem(peer - block + slices, slices)
        return pltpu.make_async_remote_copy(
            src_ref=o_buf.at[g, peer],
            dst_ref=out_ref.at[:, columns((block * kv_heads + g) * wide, wide)],
            send_sem=o_send.at[g, d - 1],
            recv_sem=o_recv.at[g, d - 1],
            device_id={"blk": peer},
            device_id_type=MESH,
        )

    def ring_copy(part, way, g, hop):
        origin = at(-hop) if way == 0 else at(hop)
        tile = kv_buf.at[part, g, origin]
        return pltpu.make_async_remote_copy(
            src_ref=tile,
            dst_ref=tile,
            send_sem=ring_send.at[part, way, g, hop],
            recv_sem=ring_recv.at[part, way, g, hop],
            device_id={"uly": ahead if way == 0 else behind},
            device_id_type=MESH,
        )

    def swap_wait(part, g):
        own_kv_copy(part, g).wait()
        for d in range(1, slices):
            swap_copy(part, g, d).wait_recv()

    def hops(way, g):
        return half if way == g % 2 else half - 1

    def poll(part, g, s):
        if s == half - 2 and g + 1 < kv_heads:
            swap_wait(part, g + 1)
        for way in range(2):
            if s > hops(way, g):
                continue
            ring_copy(part, way, g, s - 1).wait_recv()
            if s < hops(way, g):
                ring_copy(part, way, g, s).start()
            if s == hops(way, g) - 1 and g + 1 < kv_heads:
                ring_copy(part, way, g + 1, 0).start()

    for part in range(2):
        for d in range(1, slices):
            swap_copy(part, 0, d).start()
    for d in range(1, slices):
        q_copy(0, d).start()
    for part in range(2):
        swap_wait(part, 0)
        for way in range(2):
            ring_copy(part, way, 0, 0).start()
    for g in range(1, kv_heads):
        for part in range(2):
            for d in range(1, slices):
                swap_copy(part, g, d).start()
        for d in range(1, slices):
            q_copy(g, d).start()

    ends, so_far = [], 0
    for d in range(docs):
        so_far = so_far + docs_ref[d] * BLOCK
        ends.append(so_far)
    starts = []
    for b in range(slices):
        position = b * slot + me * share
        start = jnp.int32(0)
        for end in ends:
            start = jnp.where(end <= position, end, start)
        starts.append(start)

    every = range(slices)
    early, late = [b for b in every if b % 4 in (0, 3)], [b for b in every if b % 4 in (1, 2)]
    steps = [(g, s) for g in range(kv_heads) for s in range(1, half + 1)]
    polls = {t: t + 2 for t in range(len(steps) - 3)}
    for t in range(2):
        for part in range(2):
            poll(part, *steps[t])
    for t, (g, s) in enumerate(steps):
        if s == 1:
            for d in range(1, slices):
                q_copy(g, d).wait_recv()
            own_q_copy(g).wait()
            update(q_buf, kv_buf, starts, state, g, [me], me, dims, every, True)
        others = [at(-s), at(s)] if s < half else [at(half)]
        if t == len(steps) - 1:
            for part in range(2):
                poll(part, g, s)
        for part, blocks in enumerate((early, late)):
            for b in blocks:
                update(q_buf, kv_buf, starts, state, g, others, me, dims, [b], False)
                if s == half:
                    done = accum[g, b] / jnp.sum(total[g, b], axis=1, keepdims=True)
                    done = done.astype(jnp.bfloat16)
                    for h in range(group):
                        o_buf[g, b, :, h * width:(h + 1) * width] = done[
                            h * share:(h + 1) * share
                        ]
                    pl.when(b != block)(lambda g=g, b=b: o_copy(g, b).start())
            if t in polls:
                poll(part, *steps[polls[t]])
        if s == half:
            out_ref[:, columns((block * kv_heads + g) * wide, wide)] = o_buf[g, block]
    for g in range(kv_heads):
        for d in range(1, slices):
            for part in range(2):
                swap_copy(part, g, d).wait_send()
            q_copy(g, d).wait_send()
        for part in range(2):
            for way in range(2):
                for hop in range(hops(way, g)):
                    ring_copy(part, way, g, hop).wait_send()
        for d in range(1, slices):
            o_copy(g, lax.rem(block + d, slices)).wait()


def by_heads(queries, keys, values, doc_blocks, n_uly, n_blk):
    share = queries.shape[1]
    slot = share * n_uly
    kv_heads = keys.shape[2] // HEAD_WIDTH // n_blk
    group = queries.shape[2] // keys.shape[2]
    docs = doc_blocks.shape[0]
    dims = (n_blk, share, group, slot)
    vmem = pl.BlockSpec(memory_space=pltpu.VMEM)
    anywhere = pl.BlockSpec(memory_space=pl.ANY)
    rows, wide, half = group * share, group * HEAD_WIDTH, n_uly // 2
    dma = pltpu.SemaphoreType.DMA
    out = pl.pallas_call(
        functools.partial(attend, dims, n_uly, kv_heads, docs),
        out_shape=jax.ShapeDtypeStruct(queries.shape[1:], jnp.bfloat16),
        in_specs=[anywhere, anywhere, anywhere, pl.BlockSpec(memory_space=pltpu.SMEM)],
        out_specs=vmem,
        scratch_shapes=[
            pltpu.VMEM((kv_heads, n_blk, share, wide), jnp.bfloat16),
            pltpu.VMEM((2, kv_heads, n_uly, n_blk * share, HEAD_WIDTH), jnp.bfloat16),
            pltpu.VMEM((kv_heads, n_blk, share, wide), jnp.bfloat16),
            pltpu.VMEM((kv_heads, n_blk, rows, HEAD_WIDTH), jnp.float32),
            pltpu.VMEM((kv_heads, n_blk, rows, HEAD_WIDTH), jnp.float32),
            pltpu.VMEM((kv_heads, n_blk, rows, HEAD_WIDTH), jnp.float32),
            dma((2, kv_heads, n_blk - 1)),
            dma((2, kv_heads, n_blk - 1)),
            dma((kv_heads, n_blk - 1)),
            dma((kv_heads, n_blk - 1)),
            dma((2, 2, kv_heads, half)),
            dma((2, 2, kv_heads, half)),
            dma((kv_heads, n_blk - 1)),
            dma((kv_heads, n_blk - 1)),
            dma((2, kv_heads)),
            dma((kv_heads,)),
        ],
        compiler_params=pltpu.CompilerParams(
            collective_id=0, has_side_effects=True, vmem_limit_bytes=60 * 1024 * 1024
        ),
    )(queries[0], keys[0], values[0], doc_blocks)
    return out[None]


def solution(mesh):
    n_uly, n_blk = mesh.shape["uly"], mesh.shape["blk"]

    def on_device(queries, keys, values, doc_blocks):
        if (keys.shape[2] // HEAD_WIDTH) % n_blk == 0 and n_uly % 2 == 0 and n_uly > 4:
            return by_heads(queries, keys, values, doc_blocks, n_uly, n_blk)
        return general(queries, keys, values, doc_blocks)

    return jax.shard_map(
        on_device,
        mesh=mesh,
        in_specs=(
            P(("parts", "blk"), "uly", None),
            P(("parts", "blk"), "uly", None),
            P(("parts", "blk"), "uly", None),
            P("parts"),
        ),
        out_specs=P(("parts", "blk"), "uly", None),
        check_vma=False,
    )
```
